32 devices in a mesh: row: 4 (over y, core), col: 8 (over z, x).
Axes of the slice: x: 2, y: 2, z: 4, core: 2. Of those that a mesh axis runs over, the one named last changes fastest.
Arguments:
- kkt: float32 [2048, 2048], P('row', 'col'), may hold values from -4 to 4, as said below
- swaps: int32 [2, 2, 128], replicated, may hold values from 0 to 2047, as said below
- inverses: float32 [2, 256, 256], replicated
- pivots: float32 [2, 256], replicated, may hold values from -0.12 to 0.12
- couplings: float32 [2, 256], replicated, may hold values from -0.12 to 0.12
- pattern: int32 [2, 256], replicated, may hold values from 0 to 1, as said below
Outputs:
- factored: float32 [2048, 2048], P('row', 'col')
The draws below stay inside these ranges and needn't reach their ends.
Inputs may be any that keep to these rules, and one draw needn't show every extreme that they name: For panel k, swaps[k, 0, :] holds 128 distinct rows among k * 256 to k * 256 + 255, both ends of that range among them, and swaps[k, 1, :] holds 128 distinct rows among (k + 1) * 256 to 2047, both ends of that range among them. pattern[k, i] = 1 makes rows i and i + 1 one 2 x 2 block of D; no two neighbouring entries are both 1 and the last entry is 0. kkt is the stored order of a symmetric matrix.
All inputs are finite; a program needn't handle non-finite values.
Results may differ from the reference program's by a relative error of at most 0.00014.
Values sent between devices are 32-bit elements; how exact they have to be, the bound alone decides.
No kernel may reach another device: no remote copies, remote signals or barrier semaphores. Data moves between devices by JAX's collectives and lax.ppermute only.
A program may use at most 64 MiB of HBM per device.

```python
import math
import jax
import jax.numpy as jnp
from jax import lax

NB = 256
SW = 128
T_COL = 1
T_ROW = 2
N = 2048


def stored_to_global_drawn(total, tiles_dev, tile_width):
    group_total = total // (tiles_dev * tile_width)
    positions = jnp.arange(total, dtype=jnp.int32)
    tile_idx = positions // tile_width
    return (tile_idx % tiles_dev * group_total + tile_idx // tiles_dev) * tile_width + positions % tile_width


def draw_kkt(key, part):
    noise_field = jnp.clip(jax.random.normal(key, (N, N), jnp.float32), -4.0, 4.0)
    symmetric = jnp.triu(noise_field) + jnp.triu(noise_field, 1).T
    row_map = stored_to_global_drawn(N, T_ROW, NB)
    col_map = stored_to_global_drawn(N, T_COL, NB)
    return jnp.take(jnp.take(symmetric, row_map, axis=0), col_map, axis=1)


def pick_distinct(key, span, amount):
    inner = jax.random.permutation(key, span - 2)[:amount - 2].astype(jnp.int32) + 1
    chosen = jnp.concatenate([jnp.array([0, span - 1], jnp.int32), inner])
    shuffle = jax.random.permutation(jax.random.fold_in(key, 7), amount)
    return jnp.take(chosen, shuffle)


def draw_swaps(key, part):
    panels = []
    for panel in range(2):
        lead_rows = panel * NB + pick_distinct(jax.random.fold_in(key, 10 + panel), NB, SW)
        partner_rows = (panel + 1) * NB + pick_distinct(jax.random.fold_in(key, 20 + panel), N - (panel + 1) * NB, SW)
        panels.append(jnp.stack([lead_rows, partner_rows]))
    return jnp.stack(panels).astype(jnp.int32)


def draw_pattern(key, part):
    coin_flips = jax.random.randint(key, (2, NB), 0, 2, dtype=jnp.int32)
    coin_flips = coin_flips.at[:, 0].set(1).at[:, NB - 1].set(0)

    def advance(earlier, flip):
        marked = flip * (1 - earlier)
        return (marked, marked)
    _, marks = lax.scan(advance, jnp.zeros((2,), jnp.int32), coin_flips.T)
    return marks.T


def draw_inverses(key, part):
    noise_field = jnp.clip(jax.random.normal(key, (2, NB, NB), jnp.float32), -4.0, 4.0)
    return jnp.eye(NB, dtype=jnp.float32)[None, :, :] + noise_field * (0.5 / math.sqrt(NB))


def setup_inputs(seed: int = 0) -> dict:
    key_list = jax.random.split(jax.random.key(seed), 7)
    return {
        "kkt": draw_kkt(jax.random.fold_in(key_list[6], 71), 0),
        "swaps": draw_swaps(jax.random.fold_in(key_list[6], 71), 0),
        "inverses": draw_inverses(jax.random.fold_in(key_list[6], 71), 0),
        "pivots": jnp.clip(jax.random.uniform(key_list[3], (2, NB), jnp.float32, -0.12, 0.12), -0.12, 0.12),
        "couplings": jnp.clip(jax.random.uniform(key_list[4], (2, NB), jnp.float32, -0.12, 0.12), -0.12, 0.12),
        "pattern": draw_pattern(jax.random.fold_in(key_list[6], 71), 0),
    }


highest_prec = lax.Precision.HIGHEST


def stored_to_global(total, tiles_dev, tile_width):
    group_total = total // (tiles_dev * tile_width)
    positions = jnp.arange(total, dtype=jnp.int32)
    tile_idx = positions // tile_width
    return ((tile_idx % tiles_dev) * group_total + tile_idx // tiles_dev) * tile_width + positions % tile_width


def global_to_stored(total, tiles_dev, tile_width):
    group_total = total // (tiles_dev * tile_width)
    positions = jnp.arange(total, dtype=jnp.int32)
    tile_idx = positions // tile_width
    return ((tile_idx % group_total) * tiles_dev + tile_idx // group_total) * tile_width + positions % tile_width


def swap_order(lead_rows, partner_rows, total):
    row_order = jnp.arange(total, dtype=jnp.int32)
    return row_order.at[lead_rows].set(partner_rows).at[partner_rows].set(lead_rows)


def scale_cols(lower_rows, pivot_row, coupling_row, pattern_row):
    links = coupling_row * pattern_row.astype(jnp.float32)
    zero_col = jnp.zeros((lower_rows.shape[0], 1), lower_rows.dtype)
    after = jnp.concatenate([lower_rows[:, 1:], zero_col], axis=1)
    before = jnp.concatenate([zero_col, lower_rows[:, :-1]], axis=1)
    links_before = jnp.concatenate([jnp.zeros((1,), links.dtype), links[:-1]])
    return lower_rows * pivot_row + after * links + before * links_before


def reference(kkt, swaps, inverses, pivots, couplings, pattern):
    row_map = global_to_stored(N, T_ROW, NB)
    col_map = global_to_stored(N, T_COL, NB)
    matrix = jnp.take(jnp.take(kkt, row_map, axis=0), col_map, axis=1)
    tile_of = jnp.arange(N, dtype=jnp.int32) // NB
    for panel in range(2):
        row_order = swap_order(swaps[panel, 0], swaps[panel, 1], N)
        matrix = jnp.take(jnp.take(matrix, row_order, axis=0), row_order, axis=1)
        trailing = (tile_of > panel)[:, None]
        product = jnp.dot(matrix[:, panel * NB:(panel + 1) * NB], inverses[panel], precision=highest_prec, preferred_element_type=jnp.float32)
        lower_rows = jnp.where(trailing, product, 0.0)
        scaled = scale_cols(lower_rows, pivots[panel], couplings[panel], pattern[panel])
        matrix = matrix - jnp.dot(lower_rows, scaled.T, precision=highest_prec, preferred_element_type=jnp.float32)
        panel_block = jnp.where(trailing, lower_rows, matrix[:, panel * NB:(panel + 1) * NB])
        matrix = matrix.at[:, panel * NB:(panel + 1) * NB].set(panel_block)
        top_block = jnp.where(trailing.T, scaled.T, matrix[panel * NB:(panel + 1) * NB, :])
        matrix = matrix.at[panel * NB:(panel + 1) * NB, :].set(top_block)
    back_rows = stored_to_global(N, T_ROW, NB)
    back_cols = stored_to_global(N, T_COL, NB)
    return jnp.take(jnp.take(matrix, back_rows, axis=0), back_cols, axis=1)
```

```python
import functools

import jax
import jax.numpy as jnp
from jax import lax
from jax.experimental import pallas as pl
from jax.experimental.pallas import tpu as pltpu
from jax.sharding import PartitionSpec as P

f32 = jnp.float32
bf16 = jnp.bfloat16
VMEM_LIMIT = 48 * 1024 * 1024


def split(value):
    high = value.astype(bf16)
    return high, (value - high.astype(f32)).astype(bf16)


def mm(left, right, dims=(((1,), (0,)), ((), ()))):
    left_high, left_low = split(left)
    right_high, right_low = split(right)
    dot = functools.partial(lax.dot_general, dimension_numbers=dims, preferred_element_type=f32)
    return dot(left_high, right_high) + (dot(left_high, right_low) + dot(left_low, right_high))


def mm_nt(left, right):
    return mm(left, right, (((1,), (1,)), ((), ())))


def pick_rows(chosen, value):
    width = value.shape[1]
    both = jnp.dot(chosen, jnp.concatenate(split(value), axis=1), preferred_element_type=f32)
    return both[:, :width] + both[:, width:]


def pick_cols(value, chosen):
    height = value.shape[0]
    both = jnp.dot(jnp.concatenate(split(value), axis=0), chosen, preferred_element_type=f32)
    return both[:height] + both[height:]


def ones_where(mask):
    return jnp.where(mask, 1.0, 0.0).astype(bf16)


def scale(lower, factors, panel):
    pivot, link, link_before = (factors[3 * panel + i : 3 * panel + i + 1, :] for i in range(3))
    width = lower.shape[1]
    after = pltpu.roll(lower, width - 1, 1)
    before = pltpu.roll(lower, 1, 1)
    return lower * pivot + after * link + before * link_before


def call(body, outs, *args, smem=0, scratch=()):
    vmem = pl.BlockSpec(memory_space=pltpu.VMEM)
    return pl.pallas_call(
        body,
        out_shape=[jax.ShapeDtypeStruct(shape, f32) for shape in outs],
        in_specs=[pl.BlockSpec(memory_space=pltpu.SMEM)] * smem + [vmem] * (len(args) - smem),
        out_specs=[vmem] * len(outs),
        scratch_shapes=list(scratch),
        compiler_params=pltpu.CompilerParams(vmem_limit_bytes=VMEM_LIMIT),
    )(*args)


def gather_moved(me, source, row_ids, block, keep, send):
    rows = pick_rows(ones_where(source[...] == row_ids[...]), block[...])
    half = keep.shape[0]
    odd = me[2] == 1
    keep[...] = jnp.where(odd, rows[half:], rows[:half])
    send[...] = jnp.where(odd, rows[:half], rows[half:])


def place_moved(me, target, row_ids, block, mine, other, out):
    odd = me[2] == 1
    first = jnp.where(odd, other[...], mine[...])
    second = jnp.where(odd, mine[...], other[...])
    hit = row_ids[...] == target[...]
    moved = jnp.max(jnp.where(hit, 1, 0), axis=1, keepdims=True) > 0
    rows = pick_rows(ones_where(hit), jnp.concatenate([first, second], axis=0))
    out[...] = jnp.where(moved, rows, block[...])


def pick_columns(lead_tiles, source, whole, out):
    piece = out.shape[0]
    tile = whole.shape[1]
    lead = lead_tiles * tile
    wanted = source[...]
    index = lax.broadcasted_iota(jnp.int32, (tile, 1), 0)
    total = None
    for t in range(whole.shape[0] // piece):
        block = jnp.concatenate(split(whole[t * piece : (t + 1) * piece, :]), axis=0)
        part = wanted if t < lead_tiles else wanted[:, :lead]
        term = jnp.dot(block, ones_where(index + t * tile == part), preferred_element_type=f32)
        if total is None:
            total = term
        elif t < lead_tiles:
            total = total + term
        else:
            total = jnp.concatenate([total[:, :lead] + term, total[:, lead:]], axis=1)
    out[...] = total[:piece] + total[piece:]


def assemble(order, *refs):
    out = refs[-1]
    piece = refs[0].shape[0]
    for i, ref in enumerate(refs[:-1]):
        out[pl.ds(pl.multiple_of(order[i] * piece, piece), piece), :] = ref[...]


def first_panel(me, rows, target, col_ids, row_ids, block, own, inverse, factors, out, lower, lower_own):
    tile = own.shape[0]
    row, col = me[0], me[1]
    first = rows[:, :tile]
    second = rows[:, tile : 2 * tile]
    hit = target[...] == col_ids[...]
    moved = jnp.max(jnp.where(hit, 1, 0), axis=0, keepdims=True) > 0
    swapped = pick_cols(rows[:, 2 * tile :], ones_where(hit))
    matrix = jnp.where(moved, swapped, block[...])
    matrix = jnp.where(col == 0, first, jnp.where(col == 1, second, matrix))
    tail = row_ids[...] >= tile
    low = jnp.where(tail, mm(first, inverse[...]), 0.0)
    low_own = jnp.where(col > 0, mm(own[:, :tile], inverse[...]), 0.0)
    scaled = scale(low_own, factors, 0)
    matrix = matrix - mm_nt(low, scaled)
    matrix = jnp.where(jnp.logical_and(tail, col == 0), low, matrix)
    lower[...] = low
    lower_own[...] = low_own
    out[...] = matrix

    @pl.when(jnp.logical_and(row == 0, col > 0))
    def _():
        out[:tile, :] = scaled.T


def second_panel(
    me, rows, row_ids, matrix, own, lower, lower_own, corner, inverse0, inverse1, factors, out
):
    tile = own.shape[0]
    row, col = me[0], me[1]
    scaled_corner = scale(mm(corner[...], inverse0[...]), factors, 0)
    tail = row_ids[...] >= 2 * tile
    low = rows[:, tile : 2 * tile] - mm_nt(lower[...], scaled_corner)
    low = jnp.where(tail, mm(low, inverse1[...]), 0.0)
    low_own = own[:, tile : 2 * tile] - mm_nt(lower_own[...], scaled_corner)
    low_own = jnp.where(col > 1, mm(low_own, inverse1[...]), 0.0)
    scaled = scale(low_own, factors, 1)
    result = matrix[...] - mm_nt(low, scaled)
    out[...] = jnp.where(jnp.logical_and(tail, col == 1), low, result)

    @pl.when(jnp.logical_and(row == 1, col > 1))
    def _():
        out[:tile, :] = scaled.T


def through(values, leads, partners):
    hit = values[:, None] == partners[None, :]
    return jnp.where(jnp.any(hit, 1), jnp.sum(jnp.where(hit, leads[None, :], 0), 1), values)


def shards(kkt, swaps, inverses, pivots, couplings, pattern):
    height, tile = kkt.shape
    panels, _, amount = swaps.shape
    rows_axis = lax.axis_size("row")
    cols_axis = lax.axis_size("col")
    row = lax.axis_index("row")
    col = lax.axis_index("col")
    piece = height // cols_axis
    lead = panels * tile

    lead0, partner0 = swaps[0, 0], swaps[0, 1]
    lead1, partner1 = swaps[1, 0], swaps[1, 1]
    target = jnp.concatenate([lead0, partner0, lead1, partner1])
    source = jnp.concatenate(
        [partner0, lead0, through(partner1, lead0, partner0), through(lead1, lead0, partner0)]
    )
    again = jnp.any(partner0[:, None] == jnp.concatenate([lead1, partner1])[None, :], 1)
    none = jnp.full((amount,), -1, jnp.int32)
    target = jnp.concatenate([lead0, jnp.where(again, none, partner0), lead1, partner1])

    lead_ids = jnp.arange(lead, dtype=jnp.int32)
    hit = lead_ids[:, None] == target[None, :]
    lead_source = jnp.where(jnp.any(hit, 1), jnp.sum(jnp.where(hit, source[None, :], 0), 1), lead_ids)
    moved_source = jnp.concatenate([source[amount : 2 * amount], source[3 * amount :]])
    col_source = jnp.concatenate([lead_source, moved_source])[None, :]
    col_target = jnp.concatenate([target[amount : 2 * amount], target[3 * amount :]])[:, None]

    position = jnp.arange(height, dtype=jnp.int32)
    row_ids = (position // tile * rows_axis + row) * tile + position % tile
    col_ids = (col * tile + jnp.arange(tile, dtype=jnp.int32))[None, :]
    links = couplings * pattern.astype(f32)
    ends = jnp.zeros((panels, 1), f32)
    links_after = jnp.concatenate([links[:, :-1], ends], axis=1)
    links_before = jnp.concatenate([ends, links[:, :-1]], axis=1)
    factors = jnp.stack([pivots, links_after, links_before], axis=1).reshape(3 * panels, tile)
    me = jnp.stack([row, col, row % 2]).astype(jnp.int32)

    def flip(value, bit):
        return lax.ppermute(value, "row", [(i, i ^ bit) for i in range(rows_axis)])

    half = panels * amount
    keep, send = call(
        gather_moved,
        [(half, tile)] * 2,
        me,
        source[:, None],
        row_ids[None, :],
        kkt,
        smem=1,
    )
    mine = keep + flip(send, 1)
    bit = 2
    while bit < rows_axis:
        mine = mine + flip(mine, bit)
        bit *= 2
    other = flip(mine, 1)
    (block,) = call(
        place_moved,
        [(height, tile)],
        me,
        target[None, :],
        row_ids[:, None],
        kkt,
        mine,
        other,
        smem=1,
    )

    whole = lax.all_to_all(block, "col", 0, 0, tiled=True)
    (part,) = call(
        functools.partial(pick_columns, panels), [(piece, col_source.shape[1])], col_source, whole
    )
    ring = list(range(0, cols_axis, 2)) + list(range(cols_axis - 1, 0, -2))
    after = [(ring[i], ring[(i + 1) % cols_axis]) for i in range(cols_axis)]
    before = [(b, a) for a, b in after]
    right, left = part, part
    parts, steps = [part], [0]
    for step in range(1, cols_axis // 2 + 1):
        right = lax.ppermute(right, "col", after)
        parts.append(right)
        steps.append(-step)
        if step < cols_axis // 2:
            left = lax.ppermute(left, "col", before)
            parts.append(left)
            steps.append(step)
    place = jnp.where(col % 2 == 0, col // 2, cols_axis - 1 - col // 2)
    order = (place + jnp.array(steps, jnp.int32)) % cols_axis
    order = jnp.where(order < cols_axis // 2, 2 * order, 2 * (cols_axis - 1 - order) + 1)
    (rows,) = call(assemble, [(height, col_source.shape[1])], order, *parts, smem=1)

    pieces = tile // piece
    own = lax.ppermute(
        part[:, :lead],
        ("row", "col"),
        [
            (t % rows_axis * cols_axis + t // rows_axis * pieces + i, i * cols_axis + t)
            for t in range(cols_axis)
            for i in range(pieces)
        ],
    )
    own = lax.all_gather(own, "row", tiled=True)

    corner = jnp.where(row == 1, rows[:tile, :tile], 0.0)
    bit = 2
    holders = [1]
    while bit < rows_axis:
        corner = corner + lax.ppermute(corner, "row", [(i, i ^ bit) for i in holders])
        holders += [i ^ bit for i in holders]
        bit *= 2
    corner = corner + lax.ppermute(corner, "row", [(i, i ^ 1) for i in holders])

    matrix, lower, lower_own = call(
        first_panel,
        [(height, tile), (height, tile), (tile, tile)],
        me,
        rows,
        col_target,
        col_ids,
        row_ids[:, None],
        block,
        own,
        inverses[0],
        factors,
        smem=1,
    )
    (out,) = call(
        second_panel,
        [(height, tile)],
        me,
        rows,
        row_ids[:, None],
        matrix,
        own,
        lower,
        lower_own,
        corner,
        inverses[0],
        inverses[1],
        factors,
        smem=1,
    )
    return out


def solution(mesh):
    return jax.shard_map(
        shards,
        mesh=mesh,
        in_specs=(P("row", "col"), P(), P(), P(), P(), P()),
        out_specs=P("row", "col"),
        check_vma=False,
    )
```

```python
import functools

import jax
import jax.numpy as jnp
from jax import lax
from jax.experimental import pallas as pl
from jax.experimental.pallas import tpu as pltpu
from jax.sharding import PartitionSpec as P

f32 = jnp.float32
bf16 = jnp.bfloat16
VMEM_LIMIT = 20 * 1024 * 1024


def split(value):
    high = value.astype(bf16)
    return high, (value - high.astype(f32)).astype(bf16)


def mm(left, right, dims=(((1,), (0,)), ((), ()))):
    left_high, left_low = split(left)
    right_high, right_low = split(right)
    dot = functools.partial(lax.dot_general, dimension_numbers=dims, preferred_element_type=f32)
    return dot(left_high, right_high) + (dot(left_high, right_low) + dot(left_low, right_high))


def mm_nt(left, right):
    return mm(left, right, (((1,), (1,)), ((), ())))


def pick_rows(chosen, value):
    width = value.shape[1]
    both = jnp.dot(chosen, jnp.concatenate(split(value), axis=1), preferred_element_type=f32)
    return both[:, :width] + both[:, width:]


def pick_cols(value, chosen):
    height = value.shape[0]
    both = jnp.dot(jnp.concatenate(split(value), axis=0), chosen, preferred_element_type=f32)
    return both[:height] + both[height:]


def ones_where(mask):
    return jnp.where(mask, 1.0, 0.0).astype(bf16)


def scale(lower, factors, panel):
    pivot, link, link_before = (factors[3 * panel + i : 3 * panel + i + 1, :] for i in range(3))
    width = lower.shape[1]
    after = pltpu.roll(lower, width - 1, 1)
    before = pltpu.roll(lower, 1, 1)
    return lower * pivot + after * link + before * link_before


def call(body, outs, *args, smem=0, scratch=()):
    vmem = pl.BlockSpec(memory_space=pltpu.VMEM)
    return pl.pallas_call(
        body,
        out_shape=[
            jax.ShapeDtypeStruct(*out) if isinstance(out[1], type) else jax.ShapeDtypeStruct(out, f32)
            for out in outs
        ],
        in_specs=[pl.BlockSpec(memory_space=pltpu.SMEM)] * smem + [vmem] * (len(args) - smem),
        out_specs=[vmem] * len(outs),
        scratch_shapes=list(scratch),
        compiler_params=pltpu.CompilerParams(vmem_limit_bytes=VMEM_LIMIT),
    )(*args)


def row_ids(row, rows_axis, height, tile, axis):
    ids = []
    for t in range(height // tile):
        shape = (tile, 1) if axis == 0 else (1, tile)
        ids.append((t * rows_axis + row) * tile + lax.broadcasted_iota(jnp.int32, shape, axis))
    return jnp.concatenate(ids, axis=axis)


def gather_moved(rows_axis, me, swaps, block, keep, send, target_out, source_out):
    lines = swaps[...]
    height, tile = block.shape
    amount = lines.shape[1]
    upright = jnp.concatenate([lines, lines], axis=0).T
    lead0, partner0, lead1, partner1 = (lines[i : i + 1, :] for i in range(4))
    lead0_up, partner0_up, lead1_up, partner1_up = (upright[:, i : i + 1] for i in range(4))

    def through(values):
        hit = partner0_up == values
        return jnp.where(
            jnp.max(jnp.where(hit, 1, 0), axis=0, keepdims=True) > 0,
            jnp.sum(jnp.where(hit, lead0_up, 0), axis=0, keepdims=True),
            values,
        )

    def through_up(values):
        hit = values == partner0
        return jnp.where(
            jnp.max(jnp.where(hit, 1, 0), axis=1, keepdims=True) > 0,
            jnp.sum(jnp.where(hit, lead0, 0), axis=1, keepdims=True),
            values,
        )

    odd = me[2] == 1
    source1, source1_lead = through(lead1), through(partner1)
    source1_up, source1_lead_up = through_up(lead1_up), through_up(partner1_up)
    wanted = jnp.concatenate([lead0_up, partner0_up, source1_up, source1_lead_up], axis=0)
    ids = row_ids(me[0], rows_axis, height, tile, 1)
    rows = pick_rows(ones_where(wanted == ids), block[...])
    half = keep.shape[0]
    keep[...] = jnp.where(odd, rows[half:], rows[:half])
    send[...] = jnp.where(odd, rows[:half], rows[half:])

    hit = jnp.logical_or(lead1_up == partner0, partner1_up == partner0)
    again = jnp.max(jnp.where(hit, 1, 0), axis=0, keepdims=True) > 0
    target_out[...] = jnp.concatenate([lead0, jnp.where(again, -1, partner0), lead1, partner1], axis=1)

    index = lax.broadcasted_iota(jnp.int32, (1, tile), 1)

    def lead_source(ids, leads_up, sources_up):
        hit = leads_up == ids
        return jnp.where(
            jnp.max(jnp.where(hit, 1, 0), axis=0, keepdims=True) > 0,
            jnp.sum(jnp.where(hit, sources_up, 0), axis=0, keepdims=True),
            ids,
        )

    first = lead_source(index, lead0_up, partner0_up)
    second = through(lead_source(index + tile, lead1_up, partner1_up))
    source_out[...] = jnp.concatenate([first, second, lead0, source1], axis=1)


def place_moved(rows_axis, me, target, block, lead_rows, mine, other, out):
    height, tile = block.shape
    amount = target.shape[1] // 4
    odd = me[2] == 1
    first = jnp.where(odd, other[...], mine[...])
    second = jnp.where(odd, mine[...], other[...])
    aims = target[...]
    lead0, partner0, lead1, partner1 = (aims[:, i * amount : (i + 1) * amount] for i in range(4))
    lead = jnp.where(odd, lead1, lead0)
    ids = row_ids(me[0], rows_axis, height, tile, 0)
    hit = ids == jnp.concatenate([lead, partner0, partner1], axis=1)
    moved = jnp.max(jnp.where(hit, 1, 0), axis=1, keepdims=True) > 0
    rows = pick_rows(ones_where(hit), jnp.concatenate([lead_rows[...], first, second], axis=0))
    out[...] = jnp.where(moved, rows, block[...])


def pick_columns(lead_tiles, source, whole, out):
    piece = out.shape[0]
    tile = whole.shape[1]
    lead = lead_tiles * tile
    wanted = source[...]
    index = lax.broadcasted_iota(jnp.int32, (tile, 1), 0)
    total = None
    for t in range(whole.shape[0] // piece):
        block = jnp.concatenate(split(whole[t * piece : (t + 1) * piece, :]), axis=0)
        part = wanted if t < lead_tiles else wanted[:, :lead]
        term = jnp.dot(block, ones_where(index + t * tile == part), preferred_element_type=f32)
        if total is None:
            total = term
        elif t < lead_tiles:
            total = total + term
        else:
            total = jnp.concatenate([total[:, :lead] + term, total[:, lead:]], axis=1)
    out[...] = total[:piece] + total[piece:]


def first_corner(order, me, *refs):
    *pieces, out = refs
    piece = pieces[0].shape[0]
    tile = out.shape[0]
    holder = me[0] == 1

    @pl.when(jnp.logical_not(holder))
    def _():
        out[...] = jnp.zeros_like(out)

    for i, ref in enumerate(pieces):

        @pl.when(jnp.logical_and(holder, order[i] < tile // piece))
        def _(i=i, ref=ref):
            out[pl.ds(pl.multiple_of(order[i] * piece, piece), piece), :] = ref[:, :tile]


def finish(rows_axis, order, own_order, me, target, block, corner, inverses, factors, *refs):
    *pieces, out, rows, own = refs
    height, tile = block.shape
    piece = pieces[0].shape[0]
    count = height // piece
    for i, ref in enumerate(pieces):
        to, rank = (rows, order[i]) if i < count else (own, own_order[i - count])
        to[pl.ds(pl.multiple_of(rank * piece, piece), piece), :] = ref[...]

    amount = target.shape[1] // 4
    row, col = me[0], me[1]
    ids = row_ids(row, rows_axis, height, tile, 0)
    nt = (((1,), (1,)), ((), ()))

    aims = target[...]
    aims = jnp.concatenate([aims[:, amount : 2 * amount], aims[:, 3 * amount :]], axis=1)
    chosen = ones_where(col * tile + lax.broadcasted_iota(jnp.int32, (tile, 1), 0) == aims)
    ones = jnp.ones((8, 2 * amount), bf16)
    moved = lax.dot_general(ones, chosen, nt, preferred_element_type=f32)[:1] > 0.5
    swapped = jnp.concatenate(split(rows[:, 2 * tile :]), axis=0)
    swapped = lax.dot_general(swapped, chosen, nt, preferred_element_type=f32)
    swapped = swapped[:height] + swapped[height:]
    first, second = rows[:, :tile], rows[:, tile : 2 * tile]
    matrix = jnp.where(moved, swapped, block[...])
    matrix = jnp.where(col == 0, first, jnp.where(col == 1, second, matrix))

    low0 = jnp.where(ids >= tile, mm(first, inverses[0]), 0.0)
    low0_own = jnp.where(col > 0, mm(own[:, :tile], inverses[0]), 0.0)
    scaled0 = scale(low0_own, factors, 0)
    matrix = matrix - mm_nt(low0, scaled0)
    matrix = jnp.where(jnp.logical_and(ids >= tile, col == 0), low0, matrix)

    scaled_corner = scale(mm(corner[...], inverses[0]), factors, 0)
    low1 = mm(second - mm_nt(low0, scaled_corner), inverses[1])
    low1 = jnp.where(ids >= 2 * tile, low1, 0.0)
    low1_own = mm(own[:, tile : 2 * tile] - mm_nt(low0_own, scaled_corner), inverses[1])
    low1_own = jnp.where(col > 1, low1_own, 0.0)
    scaled1 = scale(low1_own, factors, 1)
    matrix = matrix - mm_nt(low1, scaled1)
    out[...] = jnp.where(jnp.logical_and(ids >= 2 * tile, col == 1), low1, matrix)

    @pl.when(jnp.logical_and(row == 0, col > 0))
    def _():
        out[:tile, :] = scaled0.T

    @pl.when(jnp.logical_and(row == 1, col > 1))
    def _():
        out[:tile, :] = scaled1.T


def shards(kkt, swaps, inverses, pivots, couplings, pattern):
    height, tile = kkt.shape
    panels, _, amount = swaps.shape
    rows_axis = lax.axis_size("row")
    cols_axis = lax.axis_size("col")
    row = lax.axis_index("row")
    col = lax.axis_index("col")
    piece = height // cols_axis
    lead = panels * tile

    links = couplings * pattern.astype(f32)
    ends = jnp.zeros((panels, 1), f32)
    links_after = jnp.concatenate([links[:, :-1], ends], axis=1)
    links_before = jnp.concatenate([ends, links[:, :-1]], axis=1)
    factors = jnp.stack([pivots, links_after, links_before], axis=1).reshape(3 * panels, tile)
    me = jnp.stack([row, col, row % 2]).astype(jnp.int32)

    def flip(value, bit):
        return lax.ppermute(value, "row", [(i, i ^ bit) for i in range(rows_axis)])

    half = 2 * amount
    keep, send, target, source = call(
        functools.partial(gather_moved, rows_axis),
        [(half, tile), (half, tile), ((1, 2 * half), jnp.int32), ((1, lead + half), jnp.int32)],
        me,
        swaps.reshape(2 * panels, amount),
        kkt,
        smem=1,
    )
    mine = keep + flip(send, 1)
    if rows_axis == 4:
        near = row < 2
        come = flip(jnp.where(near, mine[:amount], mine[amount:]), 2)
        lead_rows = mine[amount:] + come
        mine = jnp.where(near, mine[:amount], come)
    else:
        bit = 2
        while bit < rows_axis:
            mine = mine + flip(mine, bit)
            bit *= 2
        lead_rows = mine[amount:]
        mine = mine[:amount]
    other = flip(mine, 1)
    (block,) = call(
        functools.partial(place_moved, rows_axis),
        [(height, tile)],
        me,
        target,
        kkt,
        lead_rows,
        mine,
        other,
        smem=1,
    )

    whole = lax.all_to_all(block, "col", 0, 0, tiled=True)
    (part,) = call(functools.partial(pick_columns, panels), [(piece, lead + half)], source, whole)
    ring = list(range(0, cols_axis, 2)) + list(range(cols_axis - 1, 0, -2))
    after = [(ring[i], ring[(i + 1) % cols_axis]) for i in range(cols_axis)]
    before = [(b, a) for a, b in after]
    pieces = tile // piece
    right, left = part, part
    parts, steps = [part], [0]
    last = cols_axis // 2
    for step in range(1, last + 1):
        right = lax.ppermute(right, "col", after)
        parts.append(right)
        steps.append(-step)
        if step < last:
            left = lax.ppermute(left, "col", before)
            parts.append(left)
            steps.append(step)
    place = jnp.where(col % 2 == 0, col // 2, cols_axis - 1 - col // 2)
    order = (place + jnp.array(steps, jnp.int32)) % cols_axis
    order = jnp.where(order < last, 2 * order, 2 * (cols_axis - 1 - order) + 1)

    near_parts = [
        lax.ppermute(
            part[:, :lead],
            ("row", "col"),
            [
                (t % rows_axis * cols_axis + t // rows_axis * pieces + i, (i ^ bits) * cols_axis + t)
                for t in range(cols_axis)
                for i in range(pieces)
            ],
        )
        for bits in range(0, rows_axis, 2)
    ]
    own_parts = near_parts + [flip(near_part, 1) for near_part in near_parts]
    own_bits = [bits + core for core in range(2) for bits in range(0, rows_axis, 2)]
    own_order = row ^ jnp.array(own_bits, jnp.int32)

    (corner,) = call(first_corner, [(tile, tile)], order, me, *parts, smem=2)
    bit = 2
    holders = [1]
    while bit < rows_axis:
        corner = corner + lax.ppermute(corner, "row", [(i, i ^ bit) for i in holders])
        holders += [i ^ bit for i in holders]
        bit *= 2
    corner = corner + lax.ppermute(corner, "row", [(i, i ^ 1) for i in holders])

    (out,) = call(
        functools.partial(finish, rows_axis),
        [(height, tile)],
        order,
        own_order,
        me,
        target,
        block,
        corner,
        inverses,
        factors,
        *parts,
        *own_parts,
        smem=3,
        scratch=[pltpu.VMEM((height, lead + half), f32), pltpu.VMEM((tile, lead), f32)],
    )
    return out


def solution(mesh):
    return jax.shard_map(
        shards,
        mesh=mesh,
        in_specs=(P("row", "col"), P(), P(), P(), P(), P()),
        out_specs=P("row", "col"),
        check_vma=False,
    )
```

```python
import functools

import jax
import jax.numpy as jnp
from jax import lax
from jax.experimental import pallas as pl
from jax.experimental.pallas import tpu as pltpu
from jax.sharding import PartitionSpec as P

f32 = jnp.float32
bf16 = jnp.bfloat16
VMEM_LIMIT = 16 * 1024 * 1024


def split(value):
    high = value.astype(bf16)
    return high, (value - high.astype(f32)).astype(bf16)


def mm(left, right, dims=(((1,), (0,)), ((), ()))):
    left_high, left_low = split(left)
    right_high, right_low = split(right)
    dot = functools.partial(lax.dot_general, dimension_numbers=dims, preferred_element_type=f32)
    return dot(left_high, right_high) + (dot(left_high, right_low) + dot(left_low, right_high))


def mm_nt(left, right):
    return mm(left, right, (((1,), (1,)), ((), ())))


def pick_rows(chosen, value):
    width = value.shape[1]
    both = jnp.dot(chosen, jnp.concatenate(split(value), axis=1), preferred_element_type=f32)
    return both[:, :width] + both[:, width:]


def pick_cols(value, chosen):
    height = value.shape[0]
    both = jnp.dot(jnp.concatenate(split(value), axis=0), chosen, preferred_element_type=f32)
    return both[:height] + both[height:]


def ones_where(mask):
    return jnp.where(mask, 1.0, 0.0).astype(bf16)


def scale(lower, pivots, couplings, pattern, panel):
    width = lower.shape[1]
    index = lax.broadcasted_iota(jnp.int32, (1, width), 1)
    link = couplings[panel : panel + 1, :] * pattern[panel : panel + 1, :].astype(f32)
    link = jnp.where(index < width - 1, link, 0.0)
    after = pltpu.roll(lower, width - 1, 1)
    before = pltpu.roll(lower, 1, 1)
    return lower * pivots[panel : panel + 1, :] + after * link + before * pltpu.roll(link, 1, 1)


def call(body, outs, *args, smem=0, far=0, scratch=()):
    vmem = pl.BlockSpec(memory_space=pltpu.VMEM)
    return pl.pallas_call(
        body,
        out_shape=[
            jax.ShapeDtypeStruct(*out) if isinstance(out[1], type) else jax.ShapeDtypeStruct(out, f32)
            for out in outs
        ],
        in_specs=[pl.BlockSpec(memory_space=pltpu.SMEM)] * smem
        + [vmem] * (len(args) - smem - far)
        + [pl.BlockSpec(memory_space=pltpu.HBM)] * far,
        out_specs=[vmem] * len(outs),
        scratch_shapes=list(scratch),
        compiler_params=pltpu.CompilerParams(vmem_limit_bytes=VMEM_LIMIT),
    )(*args)


def row_ids(row, rows_axis, height, tile, axis):
    ids = []
    for t in range(height // tile):
        shape = (tile, 1) if axis == 0 else (1, tile)
        ids.append((t * rows_axis + row) * tile + lax.broadcasted_iota(jnp.int32, shape, axis))
    return jnp.concatenate(ids, axis=axis)


def swap_lists(swaps):
    lines = swaps[...]
    upright = jnp.concatenate([lines, lines], axis=0).T
    return [lines[i : i + 1, :] for i in range(4)], [upright[:, i : i + 1] for i in range(4)]


def either(hit, values, other, axis):
    found = jnp.max(jnp.where(hit, 1, 0), axis=axis, keepdims=True) > 0
    return jnp.where(found, jnp.sum(jnp.where(hit, values, 0), axis=axis, keepdims=True), other)


def gather_moved(rows_axis, me, swaps_far, block_far, keep, send, swaps, block, done):
    fetch_swaps = pltpu.make_async_copy(swaps_far, swaps, done.at[0])
    fetch = pltpu.make_async_copy(block_far, block, done.at[1])
    fetch_swaps.start()
    fetch.start()
    fetch_swaps.wait()
    height, tile = block.shape
    (lead0, partner0, _, _), ups = swap_lists(swaps)
    wanted = [ups[0], ups[1]] + [either(ups[i] == partner0, lead0, ups[i], 1) for i in (2, 3)]
    ids = row_ids(me[0], rows_axis, height, tile, 1)
    chosen = ones_where(jnp.concatenate(wanted, axis=0) == ids)
    fetch.wait()
    rows = pick_rows(chosen, block[...])
    half = keep.shape[0]
    odd = me[2] == 1
    keep[...] = jnp.where(odd, rows[half:], rows[:half])
    send[...] = jnp.where(odd, rows[:half], rows[half:])


def index_vectors(swaps, target, source):
    (lead0, partner0, lead1, partner1), (lead0_up, partner0_up, lead1_up, partner1_up) = swap_lists(swaps)
    hit = jnp.logical_or(lead1_up == partner0, partner1_up == partner0)
    again = jnp.max(jnp.where(hit, 1, 0), axis=0, keepdims=True) > 0
    target[...] = jnp.concatenate([lead0, jnp.where(again, -1, partner0), lead1, partner1], axis=1)
    tile = (source.shape[1] - 2 * lead0.shape[1]) // 2
    index = lax.broadcasted_iota(jnp.int32, (1, tile), 1)
    first = either(lead0_up == index, partner0_up, index, 0)
    second = either(lead1_up == index + tile, partner1_up, index + tile, 0)
    second = either(partner0_up == second, lead0_up, second, 0)
    source1 = either(partner0_up == lead1, lead0_up, lead1, 0)
    source[...] = jnp.concatenate([first, second, lead0, source1], axis=1)


def place_moved(rows_axis, me, target, block, lead_rows, mine, other, out):
    height, tile = block.shape
    amount = target.shape[1] // 4
    odd = me[2] == 1
    first = jnp.where(odd, other[...], mine[...])
    second = jnp.where(odd, mine[...], other[...])
    aims = target[...]
    lead0, partner0, lead1, partner1 = (aims[:, i * amount : (i + 1) * amount] for i in range(4))
    lead = jnp.where(odd, lead1, lead0)
    ids = row_ids(me[0], rows_axis, height, tile, 0)
    hit = ids == jnp.concatenate([lead, partner0, partner1], axis=1)
    moved = jnp.max(jnp.where(hit, 1, 0), axis=1, keepdims=True) > 0
    rows = pick_rows(ones_where(hit), jnp.concatenate([lead_rows[...], first, second], axis=0))
    out[...] = jnp.where(moved, rows, block[...])


def pick_columns(lead_tiles, source, whole, out, panel_out):
    piece = out.shape[0]
    tile = whole.shape[1]
    lead = lead_tiles * tile
    wanted = source[...]
    index = lax.broadcasted_iota(jnp.int32, (tile, 1), 0)
    total = None
    for t in range(whole.shape[0] // piece):
        block = jnp.concatenate(split(whole[t * piece : (t + 1) * piece, :]), axis=0)
        part = wanted if t < lead_tiles else wanted[:, :lead]
        term = jnp.dot(block, ones_where(index + t * tile == part), preferred_element_type=f32)
        if total is None:
            total = term
        elif t < lead_tiles:
            total = total + term
        else:
            total = jnp.concatenate([total[:, :lead] + term, total[:, lead:]], axis=1)
    total = total[:piece] + total[piece:]
    out[...] = total
    panel_out[...] = total[:, :lead]


def first_corner(order, me, *refs):
    *pieces, out = refs
    piece = pieces[0].shape[0]
    tile = out.shape[0]
    holder = me[0] == 1

    @pl.when(jnp.logical_not(holder))
    def _():
        out[...] = jnp.zeros_like(out)

    for i, ref in enumerate(pieces):

        @pl.when(jnp.logical_and(holder, order[i] < tile // piece))
        def _(i=i, ref=ref):
            out[pl.ds(pl.multiple_of(order[i] * piece, piece), piece), :] = ref[:, :tile]


def finish(
    rows_axis, order, own_order, me, target, block, inverses, pivots, couplings, pattern, *refs
):
    *pieces, out, rows, own, corner = refs
    pieces, corners = pieces[:-rows_axis], pieces[-rows_axis:]
    for i, ref in enumerate(corners):

        @pl.when(me[0] == i)
        def _(ref=ref):
            corner[...] = ref[...]

    height, tile = block.shape
    piece = pieces[0].shape[0]
    count = height // piece
    for i, ref in enumerate(pieces):
        to, rank = (rows, order[i]) if i < count else (own, own_order[i - count])
        to[pl.ds(pl.multiple_of(rank * piece, piece), piece), :] = ref[...]

    amount = target.shape[1] // 4
    row, col = me[0], me[1]
    ids = row_ids(row, rows_axis, height, tile, 0)
    nt = (((1,), (1,)), ((), ()))

    aims = target[...]
    aims = jnp.concatenate([aims[:, amount : 2 * amount], aims[:, 3 * amount :]], axis=1)
    chosen = ones_where(col * tile + lax.broadcasted_iota(jnp.int32, (tile, 1), 0) == aims)
    ones = jnp.ones((8, 2 * amount), bf16)
    moved = lax.dot_general(ones, chosen, nt, preferred_element_type=f32)[:1] > 0.5
    swapped = jnp.concatenate(split(rows[:, 2 * tile :]), axis=0)
    swapped = lax.dot_general(swapped, chosen, nt, preferred_element_type=f32)
    swapped = swapped[:height] + swapped[height:]
    first, second = rows[:, :tile], rows[:, tile : 2 * tile]
    matrix = jnp.where(moved, swapped, block[...])
    matrix = jnp.where(col == 0, first, jnp.where(col == 1, second, matrix))

    low0 = jnp.where(ids >= tile, mm(first, inverses[0]), 0.0)
    low0_own = jnp.where(col > 0, mm(own[:, :tile], inverses[0]), 0.0)
    scaled0 = scale(low0_own, pivots, couplings, pattern, 0)
    matrix = matrix - mm_nt(low0, scaled0)
    matrix = jnp.where(jnp.logical_and(ids >= tile, col == 0), low0, matrix)

    scaled_corner = scale(mm(corner[...], inverses[0]), pivots, couplings, pattern, 0)
    low1 = mm(second - mm_nt(low0, scaled_corner), inverses[1])
    low1 = jnp.where(ids >= 2 * tile, low1, 0.0)
    low1_own = mm(own[:, tile : 2 * tile] - mm_nt(low0_own, scaled_corner), inverses[1])
    low1_own = jnp.where(col > 1, low1_own, 0.0)
    scaled1 = scale(low1_own, pivots, couplings, pattern, 1)
    matrix = matrix - mm_nt(low1, scaled1)
    out[...] = jnp.where(jnp.logical_and(ids >= 2 * tile, col == 1), low1, matrix)

    @pl.when(jnp.logical_and(row == 0, col > 0))
    def _():
        out[:tile, :] = scaled0.T

    @pl.when(jnp.logical_and(row == 1, col > 1))
    def _():
        out[:tile, :] = scaled1.T


def shards(kkt, swaps, inverses, pivots, couplings, pattern):
    height, tile = kkt.shape
    panels, _, amount = swaps.shape
    rows_axis = lax.axis_size("row")
    cols_axis = lax.axis_size("col")
    row = lax.axis_index("row")
    col = lax.axis_index("col")
    piece = height // cols_axis
    lead = panels * tile

    me = jnp.stack([row, col, row % 2]).astype(jnp.int32)

    def flip(value, bit):
        return lax.ppermute(value, "row", [(i, i ^ bit) for i in range(rows_axis)])

    half = 2 * amount
    lists = swaps.reshape(2 * panels, amount)
    keep, send = call(
        functools.partial(gather_moved, rows_axis),
        [(half, tile), (half, tile)],
        me,
        lists,
        kkt,
        smem=1,
        far=2,
        scratch=[pltpu.VMEM(lists.shape, jnp.int32), pltpu.VMEM(kkt.shape, f32), pltpu.SemaphoreType.DMA((2,))],
    )
    target, source = call(
        index_vectors, [((1, 2 * half), jnp.int32), ((1, lead + half), jnp.int32)], lists
    )
    mine = keep + flip(send, 1)
    if rows_axis == 4:
        near = row < 2
        come = flip(jnp.where(near, mine[:amount], mine[amount:]), 2)
        lead_rows = mine[amount:] + come
        mine = jnp.where(near, mine[:amount], come)
    else:
        bit = 2
        while bit < rows_axis:
            mine = mine + flip(mine, bit)
            bit *= 2
        lead_rows = mine[amount:]
        mine = mine[:amount]
    other = flip(mine, 1)
    (block,) = call(
        functools.partial(place_moved, rows_axis),
        [(height, tile)],
        me,
        target,
        kkt,
        lead_rows,
        mine,
        other,
        smem=1,
    )

    whole = lax.all_to_all(block, "col", 0, 0, tiled=True)
    part, panel_part = call(
        functools.partial(pick_columns, panels), [(piece, lead + half), (piece, lead)], source, whole
    )
    ring = list(range(0, cols_axis, 2)) + list(range(cols_axis - 1, 0, -2))
    after = [(ring[i], ring[(i + 1) % cols_axis]) for i in range(cols_axis)]
    before = [(b, a) for a, b in after]
    pieces = tile // piece
    right, left = part, part
    parts, steps = [part], [0]
    last = cols_axis // 2
    for step in range(1, last + 1):
        right = lax.ppermute(right, "col", after)
        parts.append(right)
        steps.append(-step)
        if step < last:
            left = lax.ppermute(left, "col", before)
            parts.append(left)
            steps.append(step)
    place = jnp.where(col % 2 == 0, col // 2, cols_axis - 1 - col // 2)
    order = (place + jnp.array(steps, jnp.int32)) % cols_axis
    order = jnp.where(order < last, 2 * order, 2 * (cols_axis - 1 - order) + 1)

    near_parts = [
        lax.ppermute(
            panel_part,
            ("row", "col"),
            [
                (t % rows_axis * cols_axis + t // rows_axis * pieces + i, (i ^ bits) * cols_axis + t)
                for t in range(cols_axis)
                for i in range(pieces)
            ],
        )
        for bits in range(0, rows_axis, 2)
    ]
    own_parts = near_parts + [flip(near_part, 1) for near_part in near_parts]
    own_bits = [bits + core for core in range(2) for bits in range(0, rows_axis, 2)]
    own_order = row ^ jnp.array(own_bits, jnp.int32)

    (corner,) = call(first_corner, [(tile, tile)], order, me, *parts, smem=2)
    corners = [corner if r == 1 else lax.ppermute(corner, "row", [(1, r)]) for r in range(rows_axis)]
    (out,) = call(
        functools.partial(finish, rows_axis),
        [(height, tile)],
        order,
        own_order,
        me,
        target,
        block,
        inverses,
        pivots,
        couplings,
        pattern,
        *parts,
        *own_parts,
        *corners,
        smem=3,
        scratch=[
            pltpu.VMEM((height, lead + half), f32),
            pltpu.VMEM((tile, lead), f32),
            pltpu.VMEM((tile, tile), f32),
        ],
    )
    return out


def solution(mesh):
    return jax.shard_map(
        shards,
        mesh=mesh,
        in_specs=(P("row", "col"), P(), P(), P(), P(), P()),
        out_specs=P("row", "col"),
        check_vma=False,
    )
```

```python
import functools

import jax
import jax.numpy as jnp
from jax import lax
from jax.experimental import pallas as pl
from jax.experimental.pallas import tpu as pltpu
from jax.sharding import PartitionSpec as P

f32 = jnp.float32
bf16 = jnp.bfloat16
VMEM_LIMIT = 16 * 1024 * 1024


def split(value):
    high = value.astype(bf16)
    return high, (value - high.astype(f32)).astype(bf16)


def mm(left, right, dims=(((1,), (0,)), ((), ()))):
    left_high, left_low = split(left)
    right_high, right_low = split(right)
    dot = functools.partial(lax.dot_general, dimension_numbers=dims, preferred_element_type=f32)
    return dot(left_high, right_high) + (dot(left_high, right_low) + dot(left_low, right_high))


def mm_nt(left, right):
    return mm(left, right, (((1,), (1,)), ((), ())))


def pick_rows(chosen, value):
    width = value.shape[1]
    both = jnp.dot(chosen, jnp.concatenate(split(value), axis=1), preferred_element_type=f32)
    return both[:, :width] + both[:, width:]


def pick_cols(value, chosen):
    height = value.shape[0]
    both = jnp.dot(jnp.concatenate(split(value), axis=0), chosen, preferred_element_type=f32)
    return both[:height] + both[height:]


def ones_where(mask):
    return jnp.where(mask, 1.0, 0.0).astype(bf16)


def scale(lower, pivots, couplings, pattern, panel):
    width = lower.shape[1]
    index = lax.broadcasted_iota(jnp.int32, (1, width), 1)
    link = couplings[panel : panel + 1, :] * pattern[panel : panel + 1, :].astype(f32)
    link = jnp.where(index < width - 1, link, 0.0)
    after = pltpu.roll(lower, width - 1, 1)
    before = pltpu.roll(lower, 1, 1)
    return lower * pivots[panel : panel + 1, :] + after * link + before * pltpu.roll(link, 1, 1)


def call(body, outs, *args, smem=0, scratch=()):
    vmem = pl.BlockSpec(memory_space=pltpu.VMEM)
    return pl.pallas_call(
        body,
        out_shape=[
            jax.ShapeDtypeStruct(*out) if isinstance(out[1], type) else jax.ShapeDtypeStruct(out, f32)
            for out in outs
        ],
        in_specs=[pl.BlockSpec(memory_space=pltpu.SMEM)] * smem + [vmem] * (len(args) - smem),
        out_specs=[vmem] * len(outs),
        scratch_shapes=list(scratch),
        compiler_params=pltpu.CompilerParams(vmem_limit_bytes=VMEM_LIMIT),
    )(*args)


def row_ids(row, rows_axis, height, tile, axis):
    ids = []
    for t in range(height // tile):
        shape = (tile, 1) if axis == 0 else (1, tile)
        ids.append((t * rows_axis + row) * tile + lax.broadcasted_iota(jnp.int32, shape, axis))
    return jnp.concatenate(ids, axis=axis)


def swap_lists(swaps):
    lines = swaps[...]
    upright = jnp.concatenate([lines, lines], axis=0).T
    return [lines[i : i + 1, :] for i in range(4)], [upright[:, i : i + 1] for i in range(4)]


def either(hit, values, other, axis):
    found = jnp.max(jnp.where(hit, 1, 0), axis=axis, keepdims=True) > 0
    return jnp.where(found, jnp.sum(jnp.where(hit, values, 0), axis=axis, keepdims=True), other)


def gather_moved(rows_axis, me, swaps, block, keep, send):
    height, tile = block.shape
    (lead0, partner0, _, _), ups = swap_lists(swaps)
    wanted = [ups[0], ups[1]] + [either(ups[i] == partner0, lead0, ups[i], 1) for i in (2, 3)]
    ids = row_ids(me[0], rows_axis, height, tile, 1)
    chosen = ones_where(jnp.concatenate(wanted, axis=0) == ids)
    rows = pick_rows(chosen, block[...])
    half = keep.shape[0]
    odd = me[2] == 1
    keep[...] = jnp.where(odd, rows[half:], rows[:half])
    send[...] = jnp.where(odd, rows[:half], rows[half:])


def index_vectors(swaps, target, source):
    (lead0, partner0, lead1, partner1), (lead0_up, partner0_up, lead1_up, partner1_up) = swap_lists(swaps)
    hit = jnp.logical_or(lead1_up == partner0, partner1_up == partner0)
    again = jnp.max(jnp.where(hit, 1, 0), axis=0, keepdims=True) > 0
    target[...] = jnp.concatenate([lead0, jnp.where(again, -1, partner0), lead1, partner1], axis=1)
    tile = (source.shape[1] - 2 * lead0.shape[1]) // 2
    index = lax.broadcasted_iota(jnp.int32, (1, tile), 1)
    first = either(lead0_up == index, partner0_up, index, 0)
    second = either(lead1_up == index + tile, partner1_up, index + tile, 0)
    second = either(partner0_up == second, lead0_up, second, 0)
    source1 = either(partner0_up == lead1, lead0_up, lead1, 0)
    source[...] = jnp.concatenate([first, second, lead0, source1], axis=1)


def place_moved(rows_axis, me, aims_col, target, block, lead_rows, mine, other, out, *pieces):
    height, tile = block.shape
    amount = target.shape[1] // 4
    odd = me[2] == 1
    first = jnp.where(odd, other[...], mine[...])
    second = jnp.where(odd, mine[...], other[...])
    aims = target[...]
    lead0, partner0, lead1, partner1 = (aims[:, i * amount : (i + 1) * amount] for i in range(4))
    lead = jnp.where(odd, lead1, lead0)
    ids = row_ids(me[0], rows_axis, height, tile, 0)
    hit = ids == jnp.concatenate([lead, partner0, partner1], axis=1)
    moved = jnp.max(jnp.where(hit, 1, 0), axis=1, keepdims=True) > 0
    rows = pick_rows(ones_where(hit), jnp.concatenate([lead_rows[...], first, second], axis=0))
    out[...] = jnp.where(moved, rows, block[...])
    for i, ref in enumerate(pieces):
        piece = ref.shape[0]
        ref[...] = out[pl.ds(pl.multiple_of(aims_col[i] * piece, piece), piece), :]


def pick_columns(lead_tiles, me, tiles, source, inverses, *refs):
    *pieces, out, panel_out = refs
    piece, tile = pieces[0].shape
    lead = lead_tiles * tile
    wanted = source[...]
    index = lax.broadcasted_iota(jnp.int32, (tile, 1), 0)
    total = 0.0
    for i, ref in enumerate(pieces):
        block = jnp.concatenate(split(ref[...]), axis=0)
        total = total + jnp.dot(block, ones_where(index + tiles[i] * tile == wanted), preferred_element_type=f32)
    total = total[:piece] + total[piece:]
    in_first_tile = me[1] < tile // piece
    for panel in range(lead_tiles):
        place = slice(panel * tile, (panel + 1) * tile)
        plain = jnp.logical_and(me[0] == panel, in_first_tile)
        part = total[:, place]
        part = jnp.where(plain, part, mm(part, inverses[panel]))
        out[:, place] = part
        panel_out[:, place] = part
    out[:, lead:] = total[:, lead:]


def collect(rank, *refs):
    *pieces, out = refs
    piece = pieces[0].shape[0]
    count = out.shape[0] // piece
    for i, ref in enumerate(pieces):

        @pl.when(rank[i] < count)
        def _(i=i, ref=ref):
            out[pl.ds(pl.multiple_of(rank[i] * piece, piece), piece), :] = ref[:, : out.shape[1]]


def finish(
    rows_axis, order, own_order, me, target, block, inverses, pivots, couplings, pattern, *refs
):
    *pieces, out, rows, own, corner = refs
    pieces, corners = pieces[:-rows_axis], pieces[-rows_axis:]
    for i, ref in enumerate(corners):

        @pl.when(me[0] == i)
        def _(ref=ref):
            corner[...] = ref[...]

    height, tile = block.shape
    piece = pieces[0].shape[0]
    count = height // piece
    for i, ref in enumerate(pieces):
        to, rank = (rows, order[i]) if i < count else (own, own_order[i - count])
        to[pl.ds(pl.multiple_of(rank * piece, piece), piece), :] = ref[...]

    amount = target.shape[1] // 4
    row, col = me[0], me[1]
    ids = row_ids(row, rows_axis, height, tile, 0)
    nt = (((1,), (1,)), ((), ()))

    aims = target[...]
    aims = jnp.concatenate([aims[:, amount : 2 * amount], aims[:, 3 * amount :]], axis=1)
    chosen = ones_where(col * tile + lax.broadcasted_iota(jnp.int32, (tile, 1), 0) == aims)
    ones = jnp.ones((8, 2 * amount), bf16)
    moved = lax.dot_general(ones, chosen, nt, preferred_element_type=f32)[:1] > 0.5
    swapped = jnp.concatenate(split(rows[:, 2 * tile :]), axis=0)
    swapped = lax.dot_general(swapped, chosen, nt, preferred_element_type=f32)
    swapped = swapped[:height] + swapped[height:]
    first, second = rows[:, :tile], rows[:, tile : 2 * tile]
    matrix = jnp.where(moved, swapped, block[...])
    matrix = jnp.where(col == 0, first, jnp.where(col == 1, second, matrix))

    low0 = jnp.where(ids >= tile, first, 0.0)
    low0_own = jnp.where(col > 0, own[:, :tile], 0.0)
    scaled0 = scale(low0_own, pivots, couplings, pattern, 0)
    matrix = matrix - mm_nt(low0, scaled0)

    update = mm(scale(corner[...], pivots, couplings, pattern, 0).T, inverses[1])
    low1 = jnp.where(ids >= 2 * tile, second - mm(low0, update), 0.0)
    low1_own = jnp.where(col > 1, own[:, tile : 2 * tile] - mm(low0_own, update), 0.0)
    scaled1 = scale(low1_own, pivots, couplings, pattern, 1)
    matrix = matrix - mm_nt(low1, scaled1)
    out[...] = jnp.where(jnp.logical_and(ids >= 2 * tile, col == 1), low1, matrix)

    @pl.when(jnp.logical_and(row == 0, col > 0))
    def _():
        out[:tile, :] = scaled0.T

    @pl.when(jnp.logical_and(row == 1, col > 1))
    def _():
        out[:tile, :] = scaled1.T


def shards(kkt, swaps, inverses, pivots, couplings, pattern):
    height, tile = kkt.shape
    panels, _, amount = swaps.shape
    rows_axis = lax.axis_size("row")
    cols_axis = lax.axis_size("col")
    row = lax.axis_index("row")
    col = lax.axis_index("col")
    piece = height // cols_axis
    lead = panels * tile

    me = jnp.stack([row, col, row % 2]).astype(jnp.int32)

    def flip(value, bit):
        return lax.ppermute(value, "row", [(i, i ^ bit) for i in range(rows_axis)])

    half = 2 * amount
    lists = swaps.reshape(2 * panels, amount)
    keep, send = call(
        functools.partial(gather_moved, rows_axis),
        [(half, tile), (half, tile)],
        me,
        lists,
        kkt,
        smem=1,
    )
    target, source = call(
        index_vectors, [((1, 2 * half), jnp.int32), ((1, lead + half), jnp.int32)], lists
    )
    mine = keep + flip(send, 1)
    if rows_axis == 4:
        near = row < 2
        come = flip(jnp.where(near, mine[:amount], mine[amount:]), 2)
        lead_rows = mine[amount:] + come
        mine = jnp.where(near, mine[:amount], come)
    else:
        bit = 2
        while bit < rows_axis:
            mine = mine + flip(mine, bit)
            bit *= 2
        lead_rows = mine[amount:]
        mine = mine[:amount]
    other = flip(mine, 1)
    direct = cols_axis <= 8
    tiles = jnp.arange(cols_axis, dtype=jnp.int32)
    tiles = col ^ tiles if direct else tiles
    block, *pieces = call(
        functools.partial(place_moved, rows_axis),
        [(height, tile)] + [(piece, tile)] * (cols_axis if direct else 0),
        me,
        tiles,
        target,
        kkt,
        lead_rows,
        mine,
        other,
        smem=2,
    )
    if direct:
        for i in reversed(range(1, cols_axis)):
            pieces[i] = lax.ppermute(pieces[i], "col", [(c, c ^ i) for c in range(cols_axis)])
    else:
        whole = lax.all_to_all(block, "col", 0, 0, tiled=True)
        pieces = [whole[i * piece : (i + 1) * piece] for i in range(cols_axis)]
    part, panel_part = call(
        functools.partial(pick_columns, panels),
        [(piece, lead + half), (piece, lead)],
        me,
        tiles,
        source,
        inverses,
        *pieces,
        smem=2,
    )
    ring = list(range(0, cols_axis, 2)) + list(range(cols_axis - 1, 0, -2))
    after = [(ring[i], ring[(i + 1) % cols_axis]) for i in range(cols_axis)]
    before = [(b, a) for a, b in after]
    pieces = tile // piece
    near_parts = [
        lax.ppermute(
            panel_part,
            ("row", "col"),
            [
                (t % rows_axis * cols_axis + t // rows_axis * pieces + i, (i ^ bits) * cols_axis + t)
                for t in range(cols_axis)
                for i in range(pieces)
            ],
        )
        for bits in range(0, rows_axis, 2)
    ]
    right, left = part, part
    parts, steps = [part], [0]
    last = cols_axis // 2
    for step in range(1, last + 1):
        if step == last:
            right, near_parts = lax.optimization_barrier((right, near_parts))
            parts[-2] = right
        right = lax.ppermute(right, "col", after)
        parts.append(right)
        steps.append(-step)
        if step < last:
            left = lax.ppermute(left, "col", before)
            parts.append(left)
            steps.append(step)
    place = jnp.where(col % 2 == 0, col // 2, cols_axis - 1 - col // 2)
    order = (place + jnp.array(steps, jnp.int32)) % cols_axis
    order = jnp.where(order < last, 2 * order, 2 * (cols_axis - 1 - order) + 1)

    own_bits = [bits + core for core in range(2) for bits in range(0, rows_axis, 2)]
    own_order = row ^ jnp.array(own_bits, jnp.int32)

    pairs = [(cols_axis + c, cols_axis + ring[(ring.index(c) + last) % cols_axis]) for c in range(pieces)]
    extra = lax.ppermute(panel_part[:, :tile], ("row", "col"), pairs)
    (corner,) = call(collect, [(tile, tile)], order, *parts[:-1], extra, smem=1)
    corners = [corner if r == 1 else lax.ppermute(corner, "row", [(1, r)]) for r in range(rows_axis)]
    parts[-1], corners[3], near_parts = lax.optimization_barrier((parts[-1], corners[3], near_parts))
    own_parts = near_parts + [flip(near_part, 1) for near_part in near_parts]
    (out,) = call(
        functools.partial(finish, rows_axis),
        [(height, tile)],
        order,
        own_order,
        me,
        target,
        block,
        inverses,
        pivots,
        couplings,
        pattern,
        *parts,
        *own_parts,
        *corners,
        smem=3,
        scratch=[
            pltpu.VMEM((height, lead + half), f32),
            pltpu.VMEM((tile, lead), f32),
            pltpu.VMEM((tile, tile), f32),
        ],
    )
    return out


def solution(mesh):
    return jax.shard_map(
        shards,
        mesh=mesh,
        in_specs=(P("row", "col"), P(), P(), P(), P(), P()),
        out_specs=P("row", "col"),
        check_vma=False,
    )
```

```python
import functools

import jax
import jax.numpy as jnp
from jax import lax
from jax.experimental import pallas as pl
from jax.experimental.pallas import tpu as pltpu
from jax.sharding import PartitionSpec as P

f32 = jnp.float32
bf16 = jnp.bfloat16
VMEM_LIMIT = 16 * 1024 * 1024


def split(value):
    high = value.astype(bf16)
    return high, (value - high.astype(f32)).astype(bf16)


def mm(left, right, dims=(((1,), (0,)), ((), ()))):
    left_high, left_low = split(left)
    right_high, right_low = split(right)
    dot = functools.partial(lax.dot_general, dimension_numbers=dims, preferred_element_type=f32)
    return dot(left_high, right_high) + (dot(left_high, right_low) + dot(left_low, right_high))


def mm_nt(left, right):
    return mm(left, right, (((1,), (1,)), ((), ())))


def pick_rows(chosen, value):
    width = value.shape[1]
    both = jnp.dot(chosen, jnp.concatenate(split(value), axis=1), preferred_element_type=f32)
    return both[:, :width] + both[:, width:]


def pick_cols(value, chosen):
    height = value.shape[0]
    both = jnp.dot(jnp.concatenate(split(value), axis=0), chosen, preferred_element_type=f32)
    return both[:height] + both[height:]


def ones_where(mask):
    return jnp.where(mask, 1.0, 0.0).astype(bf16)


def scale(lower, pivots, couplings, pattern, panel):
    width = lower.shape[1]
    index = lax.broadcasted_iota(jnp.int32, (1, width), 1)
    link = couplings[panel : panel + 1, :] * pattern[panel : panel + 1, :].astype(f32)
    link = jnp.where(index < width - 1, link, 0.0)
    after = pltpu.roll(lower, width - 1, 1)
    before = pltpu.roll(lower, 1, 1)
    return lower * pivots[panel : panel + 1, :] + after * link + before * pltpu.roll(link, 1, 1)


def call(body, outs, *args, smem=0, scratch=()):
    vmem = pl.BlockSpec(memory_space=pltpu.VMEM)
    return pl.pallas_call(
        body,
        out_shape=[
            jax.ShapeDtypeStruct(*out) if isinstance(out[1], type) else jax.ShapeDtypeStruct(out, f32)
            for out in outs
        ],
        in_specs=[pl.BlockSpec(memory_space=pltpu.SMEM)] * smem + [vmem] * (len(args) - smem),
        out_specs=[vmem] * len(outs),
        scratch_shapes=list(scratch),
        compiler_params=pltpu.CompilerParams(vmem_limit_bytes=VMEM_LIMIT),
    )(*args)


def row_ids(row, rows_axis, height, tile, axis):
    ids = []
    for t in range(height // tile):
        shape = (tile, 1) if axis == 0 else (1, tile)
        ids.append((t * rows_axis + row) * tile + lax.broadcasted_iota(jnp.int32, shape, axis))
    return jnp.concatenate(ids, axis=axis)


def swap_lists(swaps):
    lines = swaps[...]
    upright = jnp.concatenate([lines, lines], axis=0).T
    return [lines[i : i + 1, :] for i in range(4)], [upright[:, i : i + 1] for i in range(4)]


def either(hit, values, other, axis):
    found = jnp.max(jnp.where(hit, 1, 0), axis=axis, keepdims=True) > 0
    return jnp.where(found, jnp.sum(jnp.where(hit, values, 0), axis=axis, keepdims=True), other)


def gather_moved(rows_axis, me, swaps, block, keep, send):
    height, tile = block.shape
    (lead0, partner0, _, _), ups = swap_lists(swaps)
    wanted = [ups[0], ups[1]] + [either(ups[i] == partner0, lead0, ups[i], 1) for i in (2, 3)]
    ids = row_ids(me[0], rows_axis, height, tile, 1)
    chosen = ones_where(jnp.concatenate(wanted, axis=0) == ids)
    rows = pick_rows(chosen, block[...])
    half = keep.shape[0]
    odd = me[2] == 1
    keep[...] = jnp.where(odd, rows[half:], rows[:half])
    send[...] = jnp.where(odd, rows[:half], rows[half:])


def index_vectors(swaps, inverses, target, source, high, low):
    high[...], low[...] = split(inverses[...])
    (lead0, partner0, lead1, partner1), (lead0_up, partner0_up, lead1_up, partner1_up) = swap_lists(swaps)
    hit = jnp.logical_or(lead1_up == partner0, partner1_up == partner0)
    again = jnp.max(jnp.where(hit, 1, 0), axis=0, keepdims=True) > 0
    target[...] = jnp.concatenate([lead0, jnp.where(again, -1, partner0), lead1, partner1], axis=1)
    tile = (source.shape[1] - 2 * lead0.shape[1]) // 2
    index = lax.broadcasted_iota(jnp.int32, (1, tile), 1)
    first = either(lead0_up == index, partner0_up, index, 0)
    second = either(lead1_up == index + tile, partner1_up, index + tile, 0)
    second = either(partner0_up == second, lead0_up, second, 0)
    source1 = either(partner0_up == lead1, lead0_up, lead1, 0)
    source[...] = jnp.concatenate([first, second, lead0, source1], axis=1)


def place_moved(rows_axis, me, aims_col, target, block, lead_rows, mine, other, out, *pieces):
    height, tile = block.shape
    amount = target.shape[1] // 4
    odd = me[2] == 1
    first = jnp.where(odd, other[...], mine[...])
    second = jnp.where(odd, mine[...], other[...])
    aims = target[...]
    lead0, partner0, lead1, partner1 = (aims[:, i * amount : (i + 1) * amount] for i in range(4))
    lead = jnp.where(odd, lead1, lead0)
    ids = row_ids(me[0], rows_axis, height, tile, 0)
    hit = ids == jnp.concatenate([lead, partner0, partner1], axis=1)
    moved = jnp.max(jnp.where(hit, 1, 0), axis=1, keepdims=True) > 0
    rows = pick_rows(ones_where(hit), jnp.concatenate([lead_rows[...], first, second], axis=0))
    out[...] = jnp.where(moved, rows, block[...])
    for i, ref in enumerate(pieces):
        piece = ref.shape[0]
        ref[...] = out[pl.ds(pl.multiple_of(aims_col[i] * piece, piece), piece), :]


def picked(tiles, source, pieces):
    tile = pieces[0].shape[1]
    wanted = source[...]
    index = lax.broadcasted_iota(jnp.int32, (tile, 1), 0)
    total = 0.0
    for i, ref in enumerate(pieces):
        block = jnp.concatenate(split(ref[...]), axis=0)
        total = total + jnp.dot(block, ones_where(index + tiles[i] * tile == wanted), preferred_element_type=f32)
    return total


def pick_first(tiles, source, *refs):
    *pieces, out = refs
    out[...] = picked(tiles, source, pieces)


def pick_columns(lead_tiles, me, tiles, source, high, low, so_far, *refs):
    *pieces, out, panel_out = refs
    piece, tile = pieces[0].shape
    lead = lead_tiles * tile
    total = so_far[...] + picked(tiles, source, pieces)
    total = total[:piece] + total[piece:]
    in_first_tile = me[1] < tile // piece
    for panel in range(lead_tiles):
        place = slice(panel * tile, (panel + 1) * tile)
        plain = jnp.logical_and(me[0] == panel, in_first_tile)
        part = total[:, place]
        parts = split(part)
        both = jnp.dot(jnp.concatenate(parts, axis=0), high[panel], preferred_element_type=f32)
        product = both[:piece] + (both[piece:] + jnp.dot(parts[0], low[panel], preferred_element_type=f32))
        part = jnp.where(plain, part, product)
        out[:, place] = part
        panel_out[:, place] = part
    out[:, lead:] = total[:, lead:]


def collect(rank, *refs):
    *pieces, out = refs
    piece = pieces[0].shape[0]
    count = out.shape[0] // piece
    for i, ref in enumerate(pieces):

        @pl.when(rank[i] < count)
        def _(i=i, ref=ref):
            out[pl.ds(pl.multiple_of(rank[i] * piece, piece), piece), :] = ref[:, : out.shape[1]]


def finish(
    rows_axis, order, own_order, me, target, block, inverses, pivots, couplings, pattern, *refs
):
    *pieces, out, rows, own, corner = refs
    pieces, corners = pieces[:-rows_axis], pieces[-rows_axis:]
    for i, ref in enumerate(corners):

        @pl.when(me[0] == i)
        def _(ref=ref):
            corner[...] = ref[...]

    height, tile = block.shape
    piece = pieces[0].shape[0]
    count = height // piece
    for i, ref in enumerate(pieces):
        to, rank = (rows, order[i]) if i < count else (own, own_order[i - count])
        to[pl.ds(pl.multiple_of(rank * piece, piece), piece), :] = ref[...]

    amount = target.shape[1] // 4
    row, col = me[0], me[1]
    ids = row_ids(row, rows_axis, height, tile, 0)
    nt = (((1,), (1,)), ((), ()))

    aims = target[...]
    aims = jnp.concatenate([aims[:, amount : 2 * amount], aims[:, 3 * amount :]], axis=1)
    chosen = ones_where(col * tile + lax.broadcasted_iota(jnp.int32, (tile, 1), 0) == aims)
    ones = jnp.ones((8, 2 * amount), bf16)
    moved = lax.dot_general(ones, chosen, nt, preferred_element_type=f32)[:1] > 0.5
    swapped = jnp.concatenate(split(rows[:, 2 * tile :]), axis=0)
    swapped = lax.dot_general(swapped, chosen, nt, preferred_element_type=f32)
    swapped = swapped[:height] + swapped[height:]
    first, second = rows[:, :tile], rows[:, tile : 2 * tile]
    matrix = jnp.where(moved, swapped, block[...])
    matrix = jnp.where(col == 0, first, jnp.where(col == 1, second, matrix))

    low0 = jnp.where(ids >= tile, first, 0.0)
    low0_own = jnp.where(col > 0, own[:, :tile], 0.0)
    scaled0 = scale(low0_own, pivots, couplings, pattern, 0)
    matrix = matrix - mm_nt(low0, scaled0)

    update = mm(scale(corner[...], pivots, couplings, pattern, 0).T, inverses[1])
    low1 = jnp.where(ids >= 2 * tile, second - mm(low0, update), 0.0)
    low1_own = jnp.where(col > 1, own[:, tile : 2 * tile] - mm(low0_own, update), 0.0)
    scaled1 = scale(low1_own, pivots, couplings, pattern, 1)
    matrix = matrix - mm_nt(low1, scaled1)
    out[...] = jnp.where(jnp.logical_and(ids >= 2 * tile, col == 1), low1, matrix)

    @pl.when(jnp.logical_and(row == 0, col > 0))
    def _():
        out[:tile, :] = scaled0.T

    @pl.when(jnp.logical_and(row == 1, col > 1))
    def _():
        out[:tile, :] = scaled1.T


def shards(kkt, swaps, inverses, pivots, couplings, pattern):
    height, tile = kkt.shape
    panels, _, amount = swaps.shape
    rows_axis = lax.axis_size("row")
    cols_axis = lax.axis_size("col")
    row = lax.axis_index("row")
    col = lax.axis_index("col")
    piece = height // cols_axis
    lead = panels * tile

    me = jnp.stack([row, col, row % 2]).astype(jnp.int32)

    def flip(value, bit):
        return lax.ppermute(value, "row", [(i, i ^ bit) for i in range(rows_axis)])

    half = 2 * amount
    lists = swaps.reshape(2 * panels, amount)
    keep, send = call(
        functools.partial(gather_moved, rows_axis),
        [(half, tile), (half, tile)],
        me,
        lists,
        kkt,
        smem=1,
    )
    target, source, high, low = call(
        index_vectors,
        [((1, 2 * half), jnp.int32), ((1, lead + half), jnp.int32)] + [(inverses.shape, bf16)] * 2,
        lists,
        inverses,
    )
    mine = keep + flip(send, 1)
    if rows_axis == 4:
        near = row < 2
        come = flip(jnp.where(near, mine[:amount], mine[amount:]), 2)
        lead_rows = mine[amount:] + come
        mine = jnp.where(near, mine[:amount], come)
    else:
        bit = 2
        while bit < rows_axis:
            mine = mine + flip(mine, bit)
            bit *= 2
        lead_rows = mine[amount:]
        mine = mine[:amount]
    other = flip(mine, 1)
    direct = cols_axis <= 8
    tiles = jnp.arange(cols_axis, dtype=jnp.int32)
    tiles = col ^ tiles if direct else tiles
    block, *pieces = call(
        functools.partial(place_moved, rows_axis),
        [(height, tile)] + [(piece, tile)] * (cols_axis if direct else 0),
        me,
        tiles,
        target,
        kkt,
        lead_rows,
        mine,
        other,
        smem=2,
    )
    if direct:
        for i in reversed(range(1, cols_axis)):
            pieces[i] = lax.ppermute(pieces[i], "col", [(c, c ^ i) for c in range(cols_axis)])
    else:
        whole = lax.all_to_all(block, "col", 0, 0, tiled=True)
        pieces = [whole[i * piece : (i + 1) * piece] for i in range(cols_axis)]
    near = cols_axis // 2 + 1
    (so_far,) = call(
        pick_first, [(2 * piece, lead + half)], tiles[:near], source, *pieces[:near], smem=1
    )
    part, panel_part = call(
        functools.partial(pick_columns, panels),
        [(piece, lead + half), (piece, lead)],
        me,
        tiles[near:],
        source,
        high,
        low,
        so_far,
        *pieces[near:],
        smem=2,
    )
    ring = list(range(0, cols_axis, 2)) + list(range(cols_axis - 1, 0, -2))
    after = [(ring[i], ring[(i + 1) % cols_axis]) for i in range(cols_axis)]
    before = [(b, a) for a, b in after]
    pieces = tile // piece
    near_parts = [
        lax.ppermute(
            panel_part,
            ("row", "col"),
            [
                (t % rows_axis * cols_axis + t // rows_axis * pieces + i, (i ^ bits) * cols_axis + t)
                for t in range(cols_axis)
                for i in range(pieces)
            ],
        )
        for bits in range(0, rows_axis, 2)
    ]
    right, left = part, part
    parts, steps = [part], [0]
    last = cols_axis // 2
    for step in range(1, last + 1):
        if step == last:
            right, near_parts = lax.optimization_barrier((right, near_parts))
            parts[-2] = right
        right = lax.ppermute(right, "col", after)
        parts.append(right)
        steps.append(-step)
        if step < last:
            left = lax.ppermute(left, "col", before)
            parts.append(left)
            steps.append(step)
    place = jnp.where(col % 2 == 0, col // 2, cols_axis - 1 - col // 2)
    order = (place + jnp.array(steps, jnp.int32)) % cols_axis
    order = jnp.where(order < last, 2 * order, 2 * (cols_axis - 1 - order) + 1)

    own_bits = [bits + core for core in range(2) for bits in range(0, rows_axis, 2)]
    own_order = row ^ jnp.array(own_bits, jnp.int32)

    pairs = [(cols_axis + c, cols_axis + ring[(ring.index(c) + last) % cols_axis]) for c in range(pieces)]
    extra = lax.ppermute(panel_part[:, :tile], ("row", "col"), pairs)
    (corner,) = call(collect, [(tile, tile)], order, *parts[:-1], extra, smem=1)
    corners = [corner if r == 1 else lax.ppermute(corner, "row", [(1, r)]) for r in range(rows_axis)]
    free = [flip(near_part, 1) for near_part in near_parts[:-1]]
    parts[-1], corners[3], tied = lax.optimization_barrier((parts[-1], corners[3], near_parts[-1]))
    own_parts = near_parts + free + [flip(tied, 1)]
    (out,) = call(
        functools.partial(finish, rows_axis),
        [(height, tile)],
        order,
        own_order,
        me,
        target,
        block,
        inverses,
        pivots,
        couplings,
        pattern,
        *parts,
        *own_parts,
        *corners,
        smem=3,
        scratch=[
            pltpu.VMEM((height, lead + half), f32),
            pltpu.VMEM((tile, lead), f32),
            pltpu.VMEM((tile, tile), f32),
        ],
    )
    return out


def solution(mesh):
    return jax.shard_map(
        shards,
        mesh=mesh,
        in_specs=(P("row", "col"), P(), P(), P(), P(), P()),
        out_specs=P("row", "col"),
        check_vma=False,
    )
```

```python
import functools

import jax
import jax.numpy as jnp
from jax import lax
from jax.experimental import pallas as pl
from jax.experimental.pallas import tpu as pltpu
from jax.sharding import PartitionSpec as P

f32 = jnp.float32
bf16 = jnp.bfloat16
VMEM_LIMIT = 16 * 1024 * 1024


def split(value):
    high = value.astype(bf16)
    return high, (value - high.astype(f32)).astype(bf16)


def mm(left, right, dims=(((1,), (0,)), ((), ()))):
    left_high, left_low = split(left)
    right_high, right_low = split(right)
    dot = functools.partial(lax.dot_general, dimension_numbers=dims, preferred_element_type=f32)
    return dot(left_high, right_high) + (dot(left_high, right_low) + dot(left_low, right_high))


def mm_nt(left, right):
    return mm(left, right, (((1,), (1,)), ((), ())))


def pick_rows(chosen, value):
    width = value.shape[1]
    both = jnp.dot(chosen, jnp.concatenate(split(value), axis=1), preferred_element_type=f32)
    return both[:, :width] + both[:, width:]


def pick_cols(value, chosen):
    height = value.shape[0]
    both = jnp.dot(jnp.concatenate(split(value), axis=0), chosen, preferred_element_type=f32)
    return both[:height] + both[height:]


def ones_where(mask):
    return jnp.where(mask, 1.0, 0.0).astype(bf16)


def scale(lower, pivots, couplings, pattern, panel):
    width = lower.shape[1]
    index = lax.broadcasted_iota(jnp.int32, (1, width), 1)
    link = couplings[panel : panel + 1, :] * pattern[panel : panel + 1, :].astype(f32)
    link = jnp.where(index < width - 1, link, 0.0)
    after = pltpu.roll(lower, width - 1, 1)
    before = pltpu.roll(lower, 1, 1)
    return lower * pivots[panel : panel + 1, :] + after * link + before * pltpu.roll(link, 1, 1)


def call(body, outs, *args, smem=0, scratch=()):
    vmem = pl.BlockSpec(memory_space=pltpu.VMEM)
    return pl.pallas_call(
        body,
        out_shape=[
            jax.ShapeDtypeStruct(*out) if isinstance(out[1], type) else jax.ShapeDtypeStruct(out, f32)
            for out in outs
        ],
        in_specs=[pl.BlockSpec(memory_space=pltpu.SMEM)] * smem + [vmem] * (len(args) - smem),
        out_specs=[vmem] * len(outs),
        scratch_shapes=list(scratch),
        compiler_params=pltpu.CompilerParams(vmem_limit_bytes=VMEM_LIMIT),
    )(*args)


def row_ids(row, rows_axis, height, tile, axis):
    ids = []
    for t in range(height // tile):
        shape = (tile, 1) if axis == 0 else (1, tile)
        ids.append((t * rows_axis + row) * tile + lax.broadcasted_iota(jnp.int32, shape, axis))
    return jnp.concatenate(ids, axis=axis)


def swap_lists(swaps):
    lines = swaps[...]
    upright = jnp.concatenate([lines, lines], axis=0).T
    return [lines[i : i + 1, :] for i in range(4)], [upright[:, i : i + 1] for i in range(4)]


def either(hit, values, other, axis):
    found = jnp.max(jnp.where(hit, 1, 0), axis=axis, keepdims=True) > 0
    return jnp.where(found, jnp.sum(jnp.where(hit, values, 0), axis=axis, keepdims=True), other)


def gather_moved(rows_axis, me, swaps, block, keep, send):
    height, tile = block.shape
    (lead0, partner0, _, _), ups = swap_lists(swaps)
    wanted = [ups[0], ups[1]] + [either(ups[i] == partner0, lead0, ups[i], 1) for i in (2, 3)]
    ids = row_ids(me[0], rows_axis, height, tile, 1)
    chosen = ones_where(jnp.concatenate(wanted, axis=0) == ids)
    rows = pick_rows(chosen, block[...])
    half = keep.shape[0]
    odd = me[2] == 1
    keep[...] = jnp.where(odd, rows[half:], rows[:half])
    send[...] = jnp.where(odd, rows[:half], rows[half:])


def index_vectors(swaps, inverses, target, source, high, low):
    high[...], low[...] = split(inverses[...])
    (lead0, partner0, lead1, partner1), (lead0_up, partner0_up, lead1_up, partner1_up) = swap_lists(swaps)
    hit = jnp.logical_or(lead1_up == partner0, partner1_up == partner0)
    again = jnp.max(jnp.where(hit, 1, 0), axis=0, keepdims=True) > 0
    target[...] = jnp.concatenate([lead0, jnp.where(again, -1, partner0), lead1, partner1], axis=1)
    tile = (source.shape[1] - 2 * lead0.shape[1]) // 2
    index = lax.broadcasted_iota(jnp.int32, (1, tile), 1)
    first = either(lead0_up == index, partner0_up, index, 0)
    second = either(lead1_up == index + tile, partner1_up, index + tile, 0)
    second = either(partner0_up == second, lead0_up, second, 0)
    source1 = either(partner0_up == lead1, lead0_up, lead1, 0)
    source[...] = jnp.concatenate([first, second, lead0, source1], axis=1)


def place_moved(rows_axis, me, aims_col, target, block, lead_rows, mine, other, out, *pieces):
    height, tile = block.shape
    amount = target.shape[1] // 4
    odd = me[2] == 1
    first = jnp.where(odd, other[...], mine[...])
    second = jnp.where(odd, mine[...], other[...])
    aims = target[...]
    lead0, partner0, lead1, partner1 = (aims[:, i * amount : (i + 1) * amount] for i in range(4))
    lead = jnp.where(odd, lead1, lead0)
    ids = row_ids(me[0], rows_axis, height, tile, 0)
    hit = ids == jnp.concatenate([lead, partner0, partner1], axis=1)
    moved = jnp.max(jnp.where(hit, 1, 0), axis=1, keepdims=True) > 0
    rows = pick_rows(ones_where(hit), jnp.concatenate([lead_rows[...], first, second], axis=0))
    out[...] = jnp.where(moved, rows, block[...])
    for i, ref in enumerate(pieces):
        piece = ref.shape[0]
        ref[...] = out[pl.ds(pl.multiple_of(aims_col[i] * piece, piece), piece), :]


def picked(tiles, source, pieces):
    tile = pieces[0].shape[1]
    wanted = source[...]
    index = lax.broadcasted_iota(jnp.int32, (tile, 1), 0)
    total = 0.0
    for i, ref in enumerate(pieces):
        block = jnp.concatenate(split(ref[...]), axis=0)
        total = total + jnp.dot(block, ones_where(index + tiles[i] * tile == wanted), preferred_element_type=f32)
    return total


def pick_first(tiles, source, *refs):
    *pieces, out = refs
    out[...] = picked(tiles, source, pieces)


def pick_columns(lead_tiles, me, tiles, source, high, low, so_far, *refs):
    *pieces, out, panel_out = refs
    piece, tile = pieces[0].shape
    lead = lead_tiles * tile
    total = so_far[...] + picked(tiles, source, pieces)
    total = total[:piece] + total[piece:]
    in_first_tile = me[1] < tile // piece
    for panel in range(lead_tiles):
        place = slice(panel * tile, (panel + 1) * tile)
        plain = jnp.logical_and(me[0] == panel, in_first_tile)
        part = total[:, place]
        parts = split(part)
        both = jnp.dot(jnp.concatenate(parts, axis=0), high[panel], preferred_element_type=f32)
        product = both[:piece] + (both[piece:] + jnp.dot(parts[0], low[panel], preferred_element_type=f32))
        part = jnp.where(plain, part, product)
        out[:, place] = part
        panel_out[:, place] = part
    out[:, lead:] = total[:, lead:]


def collect(rank, *refs):
    *pieces, out = refs
    piece = pieces[0].shape[0]
    count = out.shape[0] // piece
    for i, ref in enumerate(pieces):

        @pl.when(rank[i] < count)
        def _(i=i, ref=ref):
            out[pl.ds(pl.multiple_of(rank[i] * piece, piece), piece), :] = ref[:, : out.shape[1]]


def finish(
    rows_axis, order, own_order, me, target, block, inverses, pivots, couplings, pattern, *refs
):
    *pieces, out, rows, own, corner = refs
    pieces, corners = pieces[:-rows_axis], pieces[-rows_axis:]
    for i, ref in enumerate(corners):

        @pl.when(me[0] == i)
        def _(ref=ref):
            corner[...] = ref[...]

    height, tile = block.shape
    piece = pieces[0].shape[0]
    count = height // piece
    for i, ref in enumerate(pieces):
        to, rank = (rows, order[i]) if i < count else (own, own_order[i - count])
        to[pl.ds(pl.multiple_of(rank * piece, piece), piece), :] = ref[...]

    amount = target.shape[1] // 4
    row, col = me[0], me[1]
    ids = row_ids(row, rows_axis, height, tile, 0)
    nt = (((1,), (1,)), ((), ()))

    aims = target[...]
    aims = jnp.concatenate([aims[:, amount : 2 * amount], aims[:, 3 * amount :]], axis=1)
    chosen = ones_where(col * tile + lax.broadcasted_iota(jnp.int32, (tile, 1), 0) == aims)
    ones = jnp.ones((8, 2 * amount), bf16)
    moved = lax.dot_general(ones, chosen, nt, preferred_element_type=f32)[:1] > 0.5
    swapped = jnp.concatenate(split(rows[:, 2 * tile :]), axis=0)
    swapped = lax.dot_general(swapped, chosen, nt, preferred_element_type=f32)
    swapped = swapped[:height] + swapped[height:]
    first, second = rows[:, :tile], rows[:, tile : 2 * tile]
    matrix = jnp.where(moved, swapped, block[...])
    matrix = jnp.where(col == 0, first, jnp.where(col == 1, second, matrix))

    low0 = jnp.where(ids >= tile, first, 0.0)
    low0_own = jnp.where(col > 0, own[:, :tile], 0.0)
    scaled0 = scale(low0_own, pivots, couplings, pattern, 0)
    matrix = matrix - mm_nt(low0, scaled0)

    update = mm(scale(corner[...], pivots, couplings, pattern, 0).T, inverses[1])
    low1 = jnp.where(ids >= 2 * tile, second - mm(low0, update), 0.0)
    low1_own = jnp.where(col > 1, own[:, tile : 2 * tile] - mm(low0_own, update), 0.0)
    scaled1 = scale(low1_own, pivots, couplings, pattern, 1)
    matrix = matrix - mm_nt(low1, scaled1)
    out[...] = jnp.where(jnp.logical_and(ids >= 2 * tile, col == 1), low1, matrix)

    @pl.when(jnp.logical_and(row == 0, col > 0))
    def _():
        out[:tile, :] = scaled0.T

    @pl.when(jnp.logical_and(row == 1, col > 1))
    def _():
        out[:tile, :] = scaled1.T


def shards(kkt, swaps, inverses, pivots, couplings, pattern):
    height, tile = kkt.shape
    panels, _, amount = swaps.shape
    rows_axis = lax.axis_size("row")
    cols_axis = lax.axis_size("col")
    row = lax.axis_index("row")
    col = lax.axis_index("col")
    piece = height // cols_axis
    lead = panels * tile

    me = jnp.stack([row, col, row % 2]).astype(jnp.int32)

    def flip(value, bit):
        return lax.ppermute(value, "row", [(i, i ^ bit) for i in range(rows_axis)])

    half = 2 * amount
    lists = swaps.reshape(2 * panels, amount)
    keep, send = call(
        functools.partial(gather_moved, rows_axis),
        [(half, tile), (half, tile)],
        me,
        lists,
        kkt,
        smem=1,
    )
    target, source, high, low = call(
        index_vectors,
        [((1, 2 * half), jnp.int32), ((1, lead + half), jnp.int32)] + [(inverses.shape, bf16)] * 2,
        lists,
        inverses,
    )
    mine = keep + flip(send, 1)
    if rows_axis == 4:
        near = row < 2
        come = flip(jnp.where(near, mine[:amount], mine[amount:]), 2)
        lead_rows = mine[amount:] + come
        mine = jnp.where(near, mine[:amount], come)
    else:
        bit = 2
        while bit < rows_axis:
            mine = mine + flip(mine, bit)
            bit *= 2
        lead_rows = mine[amount:]
        mine = mine[:amount]
    other = flip(mine, 1)
    direct = cols_axis <= 8
    tiles = jnp.arange(cols_axis, dtype=jnp.int32)
    tiles = col ^ tiles if direct else tiles
    block, *pieces = call(
        functools.partial(place_moved, rows_axis),
        [(height, tile)] + [(piece, tile)] * (cols_axis if direct else 0),
        me,
        tiles,
        target,
        kkt,
        lead_rows,
        mine,
        other,
        smem=2,
    )
    if direct:
        for i in reversed(range(1, cols_axis)):
            pieces[i] = lax.ppermute(pieces[i], "col", [(c, c ^ i) for c in range(cols_axis)])
    else:
        whole = lax.all_to_all(block, "col", 0, 0, tiled=True)
        pieces = [whole[i * piece : (i + 1) * piece] for i in range(cols_axis)]
    near = cols_axis // 2 + 2
    (so_far,) = call(
        pick_first, [(2 * piece, lead + half)], tiles[:near], source, *pieces[:near], smem=1
    )
    part, panel_part = call(
        functools.partial(pick_columns, panels),
        [(piece, lead + half), (piece, lead)],
        me,
        tiles[near:],
        source,
        high,
        low,
        so_far,
        *pieces[near:],
        smem=2,
    )
    ring = list(range(0, cols_axis, 2)) + list(range(cols_axis - 1, 0, -2))
    after = [(ring[i], ring[(i + 1) % cols_axis]) for i in range(cols_axis)]
    before = [(b, a) for a, b in after]
    pieces = tile // piece
    near_parts = [
        lax.ppermute(
            panel_part,
            ("row", "col"),
            [
                (t % rows_axis * cols_axis + t // rows_axis * pieces + i, (i ^ bits) * cols_axis + t)
                for t in range(cols_axis)
                for i in range(pieces)
            ],
        )
        for bits in range(0, rows_axis, 2)
    ]
    right, left = part, part
    parts, steps = [part], [0]
    last = cols_axis // 2
    for step in range(1, last + 1):
        if step == last:
            right, left, near_parts = lax.optimization_barrier((right, left, near_parts))
            parts[-2:] = right, left
        right = lax.ppermute(right, "col", after)
        parts.append(right)
        steps.append(-step)
        if step < last:
            left = lax.ppermute(left, "col", before)
            parts.append(left)
            steps.append(step)
    place = jnp.where(col % 2 == 0, col // 2, cols_axis - 1 - col // 2)
    order = (place + jnp.array(steps, jnp.int32)) % cols_axis
    order = jnp.where(order < last, 2 * order, 2 * (cols_axis - 1 - order) + 1)

    own_bits = [bits + core for core in range(2) for bits in range(0, rows_axis, 2)]
    own_order = row ^ jnp.array(own_bits, jnp.int32)

    pairs = [(cols_axis + c, cols_axis + ring[(ring.index(c) + last) % cols_axis]) for c in range(pieces)]
    extra = lax.ppermute(panel_part[:, :tile], ("row", "col"), pairs)
    (corner,) = call(collect, [(tile, tile)], order, *parts[:-1], extra, smem=1)
    corners = [corner if r == 1 else lax.ppermute(corner, "row", [(1, r)]) for r in range(rows_axis)]
    free = [flip(near_part, 1) for near_part in near_parts[:-1]]
    parts[-1], corners[3], tied = lax.optimization_barrier((parts[-1], corners[3], near_parts[-1]))
    own_parts = near_parts + free + [flip(tied, 1)]
    (out,) = call(
        functools.partial(finish, rows_axis),
        [(height, tile)],
        order,
        own_order,
        me,
        target,
        block,
        inverses,
        pivots,
        couplings,
        pattern,
        *parts,
        *own_parts,
        *corners,
        smem=3,
        scratch=[
            pltpu.VMEM((height, lead + half), f32),
            pltpu.VMEM((tile, lead), f32),
            pltpu.VMEM((tile, tile), f32),
        ],
    )
    return out


def solution(mesh):
    return jax.shard_map(
        shards,
        mesh=mesh,
        in_specs=(P("row", "col"), P(), P(), P(), P(), P()),
        out_specs=P("row", "col"),
        check_vma=False,
    )
```

```python
import functools

import jax
import jax.numpy as jnp
from jax import lax
from jax.experimental import pallas as pl
from jax.experimental.pallas import tpu as pltpu
from jax.sharding import PartitionSpec as P

f32 = jnp.float32
bf16 = jnp.bfloat16
VMEM_LIMIT = 16 * 1024 * 1024


def split(value):
    high = value.astype(bf16)
    return high, (value - high.astype(f32)).astype(bf16)


def mm(left, right, dims=(((1,), (0,)), ((), ()))):
    left_high, left_low = split(left)
    right_high, right_low = split(right)
    dot = functools.partial(lax.dot_general, dimension_numbers=dims, preferred_element_type=f32)
    return dot(left_high, right_high) + (dot(left_high, right_low) + dot(left_low, right_high))


def mm_nt(left, right):
    return mm(left, right, (((1,), (1,)), ((), ())))


def pick_rows(chosen, value):
    width = value.shape[1]
    both = jnp.dot(chosen, jnp.concatenate(split(value), axis=1), preferred_element_type=f32)
    return both[:, :width] + both[:, width:]


def pick_cols(value, chosen):
    height = value.shape[0]
    both = jnp.dot(jnp.concatenate(split(value), axis=0), chosen, preferred_element_type=f32)
    return both[:height] + both[height:]


def ones_where(mask):
    return jnp.where(mask, 1.0, 0.0).astype(bf16)


def scale(lower, pivots, couplings, pattern, panel):
    width = lower.shape[1]
    index = lax.broadcasted_iota(jnp.int32, (1, width), 1)
    link = couplings[panel : panel + 1, :] * pattern[panel : panel + 1, :].astype(f32)
    link = jnp.where(index < width - 1, link, 0.0)
    after = pltpu.roll(lower, width - 1, 1)
    before = pltpu.roll(lower, 1, 1)
    return lower * pivots[panel : panel + 1, :] + after * link + before * pltpu.roll(link, 1, 1)


def call(body, outs, *args, smem=0, scratch=()):
    vmem = pl.BlockSpec(memory_space=pltpu.VMEM)
    return pl.pallas_call(
        body,
        out_shape=[
            jax.ShapeDtypeStruct(*out) if isinstance(out[1], type) else jax.ShapeDtypeStruct(out, f32)
            for out in outs
        ],
        in_specs=[pl.BlockSpec(memory_space=pltpu.SMEM)] * smem + [vmem] * (len(args) - smem),
        out_specs=[vmem] * len(outs),
        scratch_shapes=list(scratch),
        compiler_params=pltpu.CompilerParams(vmem_limit_bytes=VMEM_LIMIT),
    )(*args)


def row_ids(row, rows_axis, height, tile, axis):
    ids = []
    for t in range(height // tile):
        shape = (tile, 1) if axis == 0 else (1, tile)
        ids.append((t * rows_axis + row) * tile + lax.broadcasted_iota(jnp.int32, shape, axis))
    return jnp.concatenate(ids, axis=axis)


def swap_lists(swaps):
    lines = swaps[...]
    upright = jnp.concatenate([lines, lines], axis=0).T
    return [lines[i : i + 1, :] for i in range(4)], [upright[:, i : i + 1] for i in range(4)]


def either(hit, values, other, axis):
    found = jnp.max(jnp.where(hit, 1, 0), axis=axis, keepdims=True) > 0
    return jnp.where(found, jnp.sum(jnp.where(hit, values, 0), axis=axis, keepdims=True), other)


def gather_moved(rows_axis, me, swaps, block, keep, send):
    height, tile = block.shape
    (lead0, partner0, _, _), ups = swap_lists(swaps)
    wanted = [ups[0], ups[1]] + [either(ups[i] == partner0, lead0, ups[i], 1) for i in (2, 3)]
    ids = row_ids(me[0], rows_axis, height, tile, 1)
    chosen = ones_where(jnp.concatenate(wanted, axis=0) == ids)
    rows = pick_rows(chosen, block[...])
    half = keep.shape[0]
    odd = me[2] == 1
    keep[...] = jnp.where(odd, rows[half:], rows[:half])
    send[...] = jnp.where(odd, rows[:half], rows[half:])


def index_vectors(swaps, inverses, target, source, high, low):
    high[...], low[...] = split(inverses[...])
    (lead0, partner0, lead1, partner1), (lead0_up, partner0_up, lead1_up, partner1_up) = swap_lists(swaps)
    hit = jnp.logical_or(lead1_up == partner0, partner1_up == partner0)
    again = jnp.max(jnp.where(hit, 1, 0), axis=0, keepdims=True) > 0
    target[...] = jnp.concatenate([lead0, jnp.where(again, -1, partner0), lead1, partner1], axis=1)
    tile = (source.shape[1] - 2 * lead0.shape[1]) // 2
    index = lax.broadcasted_iota(jnp.int32, (1, tile), 1)
    first = either(lead0_up == index, partner0_up, index, 0)
    second = either(lead1_up == index + tile, partner1_up, index + tile, 0)
    second = either(partner0_up == second, lead0_up, second, 0)
    source1 = either(partner0_up == lead1, lead0_up, lead1, 0)
    source[...] = jnp.concatenate([first, second, lead0, source1], axis=1)


def place_moved(rows_axis, me, aims_col, target, block, lead_rows, mine, other, out, *pieces):
    height, tile = block.shape
    amount = target.shape[1] // 4
    odd = me[2] == 1
    first = jnp.where(odd, other[...], mine[...])
    second = jnp.where(odd, mine[...], other[...])
    aims = target[...]
    lead0, partner0, lead1, partner1 = (aims[:, i * amount : (i + 1) * amount] for i in range(4))
    lead = jnp.where(odd, lead1, lead0)
    ids = row_ids(me[0], rows_axis, height, tile, 0)
    hit = ids == jnp.concatenate([lead, partner0, partner1], axis=1)
    moved = jnp.max(jnp.where(hit, 1, 0), axis=1, keepdims=True) > 0
    rows = pick_rows(ones_where(hit), jnp.concatenate([lead_rows[...], first, second], axis=0))
    out[...] = jnp.where(moved, rows, block[...])
    for i, ref in enumerate(pieces):
        piece = ref.shape[0]
        ref[...] = out[pl.ds(pl.multiple_of(aims_col[i] * piece, piece), piece), :]


def picked(tiles, source, pieces):
    tile = pieces[0].shape[1]
    wanted = source[...]
    index = lax.broadcasted_iota(jnp.int32, (tile, 1), 0)
    total = 0.0
    for i, ref in enumerate(pieces):
        block = jnp.concatenate(split(ref[...]), axis=0)
        total = total + jnp.dot(block, ones_where(index + tiles[i] * tile == wanted), preferred_element_type=f32)
    return total


def pick_first(tiles, source, *refs):
    *pieces, out = refs
    out[...] = picked(tiles, source, pieces)


def pick_columns(lead_tiles, me, tiles, source, high, low, so_far, *refs):
    *pieces, out, panel_out = refs
    piece, tile = pieces[0].shape
    lead = lead_tiles * tile
    total = so_far[...] + picked(tiles, source, pieces)
    total = total[:piece] + total[piece:]
    in_first_tile = me[1] < tile // piece
    for panel in range(lead_tiles):
        place = slice(panel * tile, (panel + 1) * tile)
        plain = jnp.logical_and(me[0] == panel, in_first_tile)
        part = total[:, place]
        parts = split(part)
        both = jnp.dot(jnp.concatenate(parts, axis=0), high[panel], preferred_element_type=f32)
        product = both[:piece] + (both[piece:] + jnp.dot(parts[0], low[panel], preferred_element_type=f32))
        part = jnp.where(plain, part, product)
        out[:, place] = part
        panel_out[:, place] = part
    out[:, lead:] = total[:, lead:]


def collect(rank, *refs):
    *pieces, out = refs
    piece = pieces[0].shape[0]
    count = out.shape[0] // piece
    for i, ref in enumerate(pieces):

        @pl.when(rank[i] < count)
        def _(i=i, ref=ref):
            out[pl.ds(pl.multiple_of(rank[i] * piece, piece), piece), :] = ref[:, : out.shape[1]]


def finish(
    rows_axis, order, own_order, me, target, block, high, low, pivots, couplings, pattern, *refs
):
    *pieces, out, rows, own, corner = refs
    pieces, corners = pieces[:-rows_axis], pieces[-rows_axis:]
    for i, ref in enumerate(corners):

        @pl.when(me[0] == i)
        def _(ref=ref):
            corner[...] = ref[...]

    height, tile = block.shape
    piece = pieces[0].shape[0]
    count = height // piece
    for i, ref in enumerate(pieces):
        to, rank = (rows, order[i]) if i < count else (own, own_order[i - count])
        to[pl.ds(pl.multiple_of(rank * piece, piece), piece), :] = ref[...]

    amount = target.shape[1] // 4
    row, col = me[0], me[1]
    ids = row_ids(row, rows_axis, height, tile, 0)
    nt = (((1,), (1,)), ((), ()))

    aims = target[...]
    aims = jnp.concatenate([aims[:, amount : 2 * amount], aims[:, 3 * amount :]], axis=1)
    chosen = ones_where(col * tile + lax.broadcasted_iota(jnp.int32, (tile, 1), 0) == aims)
    ones = jnp.ones((8, 2 * amount), bf16)
    moved = lax.dot_general(ones, chosen, nt, preferred_element_type=f32)[:1] > 0.5
    swapped = jnp.concatenate(split(rows[:, 2 * tile :]), axis=0)
    swapped = lax.dot_general(swapped, chosen, nt, preferred_element_type=f32)
    swapped = swapped[:height] + swapped[height:]
    first, second = rows[:, :tile], rows[:, tile : 2 * tile]
    matrix = jnp.where(moved, swapped, block[...])
    matrix = jnp.where(col == 0, first, jnp.where(col == 1, second, matrix))

    low0 = jnp.where(ids >= tile, first, 0.0)
    low0_own = jnp.where(col > 0, own[:, :tile], 0.0)
    scaled0 = scale(low0_own, pivots, couplings, pattern, 0)
    matrix = matrix - mm_nt(low0, scaled0)

    parts = split(scale(corner[...], pivots, couplings, pattern, 0).T)
    both = jnp.dot(jnp.concatenate(parts, axis=0), high[1], preferred_element_type=f32)
    update = both[:tile] + (both[tile:] + jnp.dot(parts[0], low[1], preferred_element_type=f32))
    low1 = jnp.where(ids >= 2 * tile, second - mm(low0, update), 0.0)
    low1_own = jnp.where(col > 1, own[:, tile : 2 * tile] - mm(low0_own, update), 0.0)
    scaled1 = scale(low1_own, pivots, couplings, pattern, 1)
    matrix = matrix - mm_nt(low1, scaled1)
    out[...] = jnp.where(jnp.logical_and(ids >= 2 * tile, col == 1), low1, matrix)

    @pl.when(jnp.logical_and(row == 0, col > 0))
    def _():
        out[:tile, :] = scaled0.T

    @pl.when(jnp.logical_and(row == 1, col > 1))
    def _():
        out[:tile, :] = scaled1.T


def shards(kkt, swaps, inverses, pivots, couplings, pattern):
    height, tile = kkt.shape
    panels, _, amount = swaps.shape
    rows_axis = lax.axis_size("row")
    cols_axis = lax.axis_size("col")
    row = lax.axis_index("row")
    col = lax.axis_index("col")
    piece = height // cols_axis
    lead = panels * tile

    me = jnp.stack([row, col, row % 2]).astype(jnp.int32)

    def flip(value, bit):
        return lax.ppermute(value, "row", [(i, i ^ bit) for i in range(rows_axis)])

    half = 2 * amount
    lists = swaps.reshape(2 * panels, amount)
    keep, send = call(
        functools.partial(gather_moved, rows_axis),
        [(half, tile), (half, tile)],
        me,
        lists,
        kkt,
        smem=1,
    )
    target, source, high, low = call(
        index_vectors,
        [((1, 2 * half), jnp.int32), ((1, lead + half), jnp.int32)] + [(inverses.shape, bf16)] * 2,
        lists,
        inverses,
    )
    mine = keep + flip(send, 1)
    if rows_axis == 4:
        near = row < 2
        come = flip(jnp.where(near, mine[:amount], mine[amount:]), 2)
        lead_rows = mine[amount:] + come
        mine = jnp.where(near, mine[:amount], come)
    else:
        bit = 2
        while bit < rows_axis:
            mine = mine + flip(mine, bit)
            bit *= 2
        lead_rows = mine[amount:]
        mine = mine[:amount]
    other = flip(mine, 1)
    direct = cols_axis <= 8
    tiles = jnp.arange(cols_axis, dtype=jnp.int32)
    tiles = col ^ tiles if direct else tiles
    block, *pieces = call(
        functools.partial(place_moved, rows_axis),
        [(height, tile)] + [(piece, tile)] * (cols_axis if direct else 0),
        me,
        tiles,
        target,
        kkt,
        lead_rows,
        mine,
        other,
        smem=2,
    )
    if direct:
        for i in reversed(range(1, cols_axis)):
            pieces[i] = lax.ppermute(pieces[i], "col", [(c, c ^ i) for c in range(cols_axis)])
    else:
        whole = lax.all_to_all(block, "col", 0, 0, tiled=True)
        pieces = [whole[i * piece : (i + 1) * piece] for i in range(cols_axis)]
    near = cols_axis // 2 + 1
    (so_far,) = call(
        pick_first, [(2 * piece, lead + half)], tiles[:near], source, *pieces[:near], smem=1
    )
    part, panel_part = call(
        functools.partial(pick_columns, panels),
        [(piece, lead + half), (piece, lead)],
        me,
        tiles[near:],
        source,
        high,
        low,
        so_far,
        *pieces[near:],
        smem=2,
    )
    ring = list(range(0, cols_axis, 2)) + list(range(cols_axis - 1, 0, -2))
    after = [(ring[i], ring[(i + 1) % cols_axis]) for i in range(cols_axis)]
    before = [(b, a) for a, b in after]
    pieces = tile // piece
    near_parts = [
        lax.ppermute(
            panel_part,
            ("row", "col"),
            [
                (t % rows_axis * cols_axis + t // rows_axis * pieces + i, (i ^ bits) * cols_axis + t)
                for t in range(cols_axis)
                for i in range(pieces)
            ],
        )
        for bits in range(0, rows_axis, 2)
    ]
    right, left = part, part
    parts, steps = [part], [0]
    last = cols_axis // 2
    for step in range(1, last + 1):
        if step == last:
            right, near_parts = lax.optimization_barrier((right, near_parts))
            parts[-2] = right
        right = lax.ppermute(right, "col", after)
        parts.append(right)
        steps.append(-step)
        if step < last:
            left = lax.ppermute(left, "col", before)
            parts.append(left)
            steps.append(step)
    place = jnp.where(col % 2 == 0, col // 2, cols_axis - 1 - col // 2)
    order = (place + jnp.array(steps, jnp.int32)) % cols_axis
    order = jnp.where(order < last, 2 * order, 2 * (cols_axis - 1 - order) + 1)

    own_bits = [bits + core for core in range(2) for bits in range(0, rows_axis, 2)]
    own_order = row ^ jnp.array(own_bits, jnp.int32)

    pairs = [(cols_axis + c, cols_axis + ring[(ring.index(c) + last) % cols_axis]) for c in range(pieces)]
    extra = lax.ppermute(panel_part[:, :tile], ("row", "col"), pairs)
    (corner,) = call(collect, [(tile, tile)], order, *parts[:-1], extra, smem=1)
    corners = [corner if r == 1 else lax.ppermute(corner, "row", [(1, r)]) for r in range(rows_axis)]
    free = [flip(near_part, 1) for near_part in near_parts[:-1]]
    parts[-1], corners[3], tied = lax.optimization_barrier((parts[-1], corners[3], near_parts[-1]))
    own_parts = near_parts + free + [flip(tied, 1)]
    (out,) = call(
        functools.partial(finish, rows_axis),
        [(height, tile)],
        order,
        own_order,
        me,
        target,
        block,
        high,
        low,
        pivots,
        couplings,
        pattern,
        *parts,
        *own_parts,
        *corners,
        smem=3,
        scratch=[
            pltpu.VMEM((height, lead + half), f32),
            pltpu.VMEM((tile, lead), f32),
            pltpu.VMEM((tile, tile), f32),
        ],
    )
    return out


def solution(mesh):
    return jax.shard_map(
        shards,
        mesh=mesh,
        in_specs=(P("row", "col"), P(), P(), P(), P(), P()),
        out_specs=P("row", "col"),
        check_vma=False,
    )
```

```python
import functools

import jax
import jax.numpy as jnp
from jax import lax
from jax.experimental import pallas as pl
from jax.experimental.pallas import tpu as pltpu
from jax.sharding import PartitionSpec as P

f32 = jnp.float32
bf16 = jnp.bfloat16
VMEM_LIMIT = 16 * 1024 * 1024


def split(value):
    high = value.astype(bf16)
    return high, (value - high.astype(f32)).astype(bf16)


def mm(left, right, dims=(((1,), (0,)), ((), ()))):
    left_high, left_low = split(left)
    right_high, right_low = split(right)
    dot = functools.partial(lax.dot_general, dimension_numbers=dims, preferred_element_type=f32)
    return dot(left_high, right_high) + (dot(left_high, right_low) + dot(left_low, right_high))


def mm_nt(left, right):
    return mm(left, right, (((1,), (1,)), ((), ())))


def pick_rows(chosen, value):
    width = value.shape[1]
    both = jnp.dot(chosen, jnp.concatenate(split(value), axis=1), preferred_element_type=f32)
    return both[:, :width] + both[:, width:]


def pick_cols(value, chosen):
    height = value.shape[0]
    both = jnp.dot(jnp.concatenate(split(value), axis=0), chosen, preferred_element_type=f32)
    return both[:height] + both[height:]


def ones_where(mask):
    return jnp.where(mask, 1.0, 0.0).astype(bf16)


def scale(lower, pivots, couplings, pattern, panel):
    width = lower.shape[1]
    index = lax.broadcasted_iota(jnp.int32, (1, width), 1)
    link = couplings[panel : panel + 1, :] * pattern[panel : panel + 1, :].astype(f32)
    link = jnp.where(index < width - 1, link, 0.0)
    after = pltpu.roll(lower, width - 1, 1)
    before = pltpu.roll(lower, 1, 1)
    return lower * pivots[panel : panel + 1, :] + after * link + before * pltpu.roll(link, 1, 1)


def call(body, outs, *args, smem=0, scratch=()):
    vmem = pl.BlockSpec(memory_space=pltpu.VMEM)
    return pl.pallas_call(
        body,
        out_shape=[
            jax.ShapeDtypeStruct(*out) if isinstance(out[1], type) else jax.ShapeDtypeStruct(out, f32)
            for out in outs
        ],
        in_specs=[pl.BlockSpec(memory_space=pltpu.SMEM)] * smem + [vmem] * (len(args) - smem),
        out_specs=[vmem] * len(outs),
        scratch_shapes=list(scratch),
        compiler_params=pltpu.CompilerParams(vmem_limit_bytes=VMEM_LIMIT),
    )(*args)


def row_ids(row, rows_axis, height, tile, axis):
    ids = []
    for t in range(height // tile):
        shape = (tile, 1) if axis == 0 else (1, tile)
        ids.append((t * rows_axis + row) * tile + lax.broadcasted_iota(jnp.int32, shape, axis))
    return jnp.concatenate(ids, axis=axis)


def swap_lists(swaps):
    lines = swaps[...]
    upright = jnp.concatenate([lines, lines], axis=0).T
    return [lines[i : i + 1, :] for i in range(4)], [upright[:, i : i + 1] for i in range(4)]


def either(hit, values, other, axis):
    found = jnp.max(jnp.where(hit, 1, 0), axis=axis, keepdims=True) > 0
    return jnp.where(found, jnp.sum(jnp.where(hit, values, 0), axis=axis, keepdims=True), other)


def gather_moved(rows_axis, me, swaps, block, keep, send):
    height, tile = block.shape
    (lead0, partner0, _, _), ups = swap_lists(swaps)
    wanted = [ups[0], ups[1]] + [either(ups[i] == partner0, lead0, ups[i], 1) for i in (2, 3)]
    ids = row_ids(me[0], rows_axis, height, tile, 1)
    chosen = ones_where(jnp.concatenate(wanted, axis=0) == ids)
    rows = pick_rows(chosen, block[...])
    half = keep.shape[0]
    odd = me[2] == 1
    keep[...] = jnp.where(odd, rows[half:], rows[:half])
    send[...] = jnp.where(odd, rows[:half], rows[half:])


def index_vectors(swaps, inverses, target, source, high, low):
    high[...], low[...] = split(inverses[...])
    (lead0, partner0, lead1, partner1), (lead0_up, partner0_up, lead1_up, partner1_up) = swap_lists(swaps)
    hit = jnp.logical_or(lead1_up == partner0, partner1_up == partner0)
    again = jnp.max(jnp.where(hit, 1, 0), axis=0, keepdims=True) > 0
    target[...] = jnp.concatenate([lead0, jnp.where(again, -1, partner0), lead1, partner1], axis=1)
    tile = (source.shape[1] - 2 * lead0.shape[1]) // 2
    index = lax.broadcasted_iota(jnp.int32, (1, tile), 1)
    first = either(lead0_up == index, partner0_up, index, 0)
    second = either(lead1_up == index + tile, partner1_up, index + tile, 0)
    second = either(partner0_up == second, lead0_up, second, 0)
    source1 = either(partner0_up == lead1, lead0_up, lead1, 0)
    source[...] = jnp.concatenate([first, second, lead0, source1], axis=1)


def place_moved(rows_axis, me, aims_col, target, block, lead_rows, mine, other, out, *pieces):
    height, tile = block.shape
    amount = target.shape[1] // 4
    odd = me[2] == 1
    first = jnp.where(odd, other[...], mine[...])
    second = jnp.where(odd, mine[...], other[...])
    aims = target[...]
    lead0, partner0, lead1, partner1 = (aims[:, i * amount : (i + 1) * amount] for i in range(4))
    lead = jnp.where(odd, lead1, lead0)
    ids = row_ids(me[0], rows_axis, height, tile, 0)
    hit = ids == jnp.concatenate([lead, partner0, partner1], axis=1)
    moved = jnp.max(jnp.where(hit, 1, 0), axis=1, keepdims=True) > 0
    rows = pick_rows(ones_where(hit), jnp.concatenate([lead_rows[...], first, second], axis=0))
    out[...] = jnp.where(moved, rows, block[...])
    for i, ref in enumerate(pieces):
        piece = ref.shape[0]
        ref[...] = out[pl.ds(pl.multiple_of(aims_col[i] * piece, piece), piece), :]


def picked(tiles, source, pieces):
    tile = pieces[0].shape[1]
    wanted = source[...]
    index = lax.broadcasted_iota(jnp.int32, (tile, 1), 0)
    total = 0.0
    for i, ref in enumerate(pieces):
        block = jnp.concatenate(split(ref[...]), axis=0)
        total = total + jnp.dot(block, ones_where(index + tiles[i] * tile == wanted), preferred_element_type=f32)
    return total


def pick_first(tiles, source, *refs):
    *pieces, out = refs
    out[...] = picked(tiles, source, pieces)


def pick_columns(lead_tiles, me, tiles, source, high, low, so_far, *refs):
    *pieces, out, panel_out = refs
    piece, tile = pieces[0].shape
    lead = lead_tiles * tile
    total = so_far[...] + picked(tiles, source, pieces)
    total = total[:piece] + total[piece:]
    in_first_tile = me[1] < tile // piece
    for panel in range(lead_tiles):
        place = slice(panel * tile, (panel + 1) * tile)
        plain = jnp.logical_and(me[0] == panel, in_first_tile)
        part = total[:, place]
        parts = split(part)
        both = jnp.dot(jnp.concatenate(parts, axis=0), high[panel], preferred_element_type=f32)
        product = both[:piece] + (both[piece:] + jnp.dot(parts[0], low[panel], preferred_element_type=f32))
        part = jnp.where(plain, part, product)
        out[:, place] = part
        panel_out[:, place] = part
    out[:, lead:] = total[:, lead:]


def collect(rank, *refs):
    *pieces, out = refs
    piece = pieces[0].shape[0]
    count = out.shape[0] // piece
    for i, ref in enumerate(pieces):

        @pl.when(rank[i] < count)
        def _(i=i, ref=ref):
            out[pl.ds(pl.multiple_of(rank[i] * piece, piece), piece), :] = ref[:, : out.shape[1]]


def finish(
    rows_axis, order, own_order, me, target, block, inverses, pivots, couplings, pattern, *refs
):
    *pieces, out, rows, own, corner = refs
    pieces, corners = pieces[:-rows_axis], pieces[-rows_axis:]
    for i, ref in enumerate(corners):

        @pl.when(me[0] == i)
        def _(ref=ref):
            corner[...] = ref[...]

    height, tile = block.shape
    piece = pieces[0].shape[0]
    count = height // piece
    for i, ref in enumerate(pieces):
        to, rank = (rows, order[i]) if i < count else (own, own_order[i - count])
        to[pl.ds(pl.multiple_of(rank * piece, piece), piece), :] = ref[...]

    amount = target.shape[1] // 4
    row, col = me[0], me[1]
    ids = row_ids(row, rows_axis, height, tile, 0)
    nt = (((1,), (1,)), ((), ()))

    aims = target[...]
    aims = jnp.concatenate([aims[:, amount : 2 * amount], aims[:, 3 * amount :]], axis=1)
    chosen = ones_where(col * tile + lax.broadcasted_iota(jnp.int32, (tile, 1), 0) == aims)
    ones = jnp.ones((8, 2 * amount), bf16)
    moved = lax.dot_general(ones, chosen, nt, preferred_element_type=f32)[:1] > 0.5
    swapped = jnp.concatenate(split(rows[:, 2 * tile :]), axis=0)
    swapped = lax.dot_general(swapped, chosen, nt, preferred_element_type=f32)
    swapped = swapped[:height] + swapped[height:]
    first, second = rows[:, :tile], rows[:, tile : 2 * tile]
    matrix = jnp.where(moved, swapped, block[...])
    matrix = jnp.where(col == 0, first, jnp.where(col == 1, second, matrix))

    low0 = jnp.where(ids >= tile, first, 0.0)
    low0_own = jnp.where(col > 0, own[:, :tile], 0.0)
    scaled0 = scale(low0_own, pivots, couplings, pattern, 0)
    matrix = matrix - mm_nt(low0, scaled0)

    update = mm(scale(corner[...], pivots, couplings, pattern, 0).T, inverses[1])
    low1 = jnp.where(ids >= 2 * tile, second - mm(low0, update), 0.0)
    low1_own = jnp.where(col > 1, own[:, tile : 2 * tile] - mm(low0_own, update), 0.0)
    scaled1 = scale(low1_own, pivots, couplings, pattern, 1)
    matrix = matrix - mm_nt(low1, scaled1)
    out[...] = jnp.where(jnp.logical_and(ids >= 2 * tile, col == 1), low1, matrix)

    @pl.when(jnp.logical_and(row == 0, col > 0))
    def _():
        out[:tile, :] = scaled0.T

    @pl.when(jnp.logical_and(row == 1, col > 1))
    def _():
        out[:tile, :] = scaled1.T


def shards(kkt, swaps, inverses, pivots, couplings, pattern):
    height, tile = kkt.shape
    panels, _, amount = swaps.shape
    rows_axis = lax.axis_size("row")
    cols_axis = lax.axis_size("col")
    row = lax.axis_index("row")
    col = lax.axis_index("col")
    piece = height // cols_axis
    lead = panels * tile

    me = jnp.stack([row, col, row % 2]).astype(jnp.int32)

    def flip(value, bit):
        return lax.ppermute(value, "row", [(i, i ^ bit) for i in range(rows_axis)])

    half = 2 * amount
    lists = swaps.reshape(2 * panels, amount)
    keep, send = call(
        functools.partial(gather_moved, rows_axis),
        [(half, tile), (half, tile)],
        me,
        lists,
        kkt,
        smem=1,
    )
    target, source, high, low = call(
        index_vectors,
        [((1, 2 * half), jnp.int32), ((1, lead + half), jnp.int32)] + [(inverses.shape, bf16)] * 2,
        lists,
        inverses,
    )
    mine = keep + flip(send, 1)
    if rows_axis == 4:
        near = row < 2
        come = flip(jnp.where(near, mine[:amount], mine[amount:]), 2)
        lead_rows = mine[amount:] + come
        mine = jnp.where(near, mine[:amount], come)
    else:
        bit = 2
        while bit < rows_axis:
            mine = mine + flip(mine, bit)
            bit *= 2
        lead_rows = mine[amount:]
        mine = mine[:amount]
    other = flip(mine, 1)
    direct = cols_axis <= 8
    tiles = jnp.arange(cols_axis, dtype=jnp.int32)
    tiles = col ^ tiles if direct else tiles
    block, *pieces = call(
        functools.partial(place_moved, rows_axis),
        [(height, tile)] + [(piece, tile)] * (cols_axis if direct else 0),
        me,
        tiles,
        target,
        kkt,
        lead_rows,
        mine,
        other,
        smem=2,
    )
    if direct:
        for i in reversed(range(1, cols_axis)):
            pieces[i] = lax.ppermute(pieces[i], "col", [(c, c ^ i) for c in range(cols_axis)])
    else:
        whole = lax.all_to_all(block, "col", 0, 0, tiled=True)
        pieces = [whole[i * piece : (i + 1) * piece] for i in range(cols_axis)]
    near = cols_axis // 2 + 1
    (so_far,) = call(
        pick_first, [(2 * piece, lead + half)], tiles[:near], source, *pieces[:near], smem=1
    )
    part, panel_part = call(
        functools.partial(pick_columns, panels),
        [(piece, lead + half), (piece, lead)],
        me,
        tiles[near:],
        source,
        high,
        low,
        so_far,
        *pieces[near:],
        smem=2,
    )
    ring = list(range(0, cols_axis, 2)) + list(range(cols_axis - 1, 0, -2))
    after = [(ring[i], ring[(i + 1) % cols_axis]) for i in range(cols_axis)]
    before = [(b, a) for a, b in after]
    pieces = tile // piece
    near_parts = [
        lax.ppermute(
            panel_part,
            ("row", "col"),
            [
                (t % rows_axis * cols_axis + t // rows_axis * pieces + i, (i ^ bits) * cols_axis + t)
                for t in range(cols_axis)
                for i in range(pieces)
            ],
        )
        for bits in range(0, rows_axis, 2)
    ]
    right, left = part, part
    parts, steps = [part], [0]
    last = cols_axis // 2
    for step in range(1, last + 1):
        if step == last:
            right, near_parts = lax.optimization_barrier((right, near_parts))
            parts[-2] = right
        right = lax.ppermute(right, "col", after)
        parts.append(right)
        steps.append(-step)
        if step < last:
            left = lax.ppermute(left, "col", before)
            parts.append(left)
            steps.append(step)
    place = jnp.where(col % 2 == 0, col // 2, cols_axis - 1 - col // 2)
    order = (place + jnp.array(steps, jnp.int32)) % cols_axis
    order = jnp.where(order < last, 2 * order, 2 * (cols_axis - 1 - order) + 1)

    own_bits = [bits + core for core in range(2) for bits in range(0, rows_axis, 2)]
    own_order = row ^ jnp.array(own_bits, jnp.int32)

    pairs = [(cols_axis + c, cols_axis + ring[(ring.index(c) + last) % cols_axis]) for c in range(pieces)]
    extra = lax.ppermute(panel_part[:, :tile], ("row", "col"), pairs)
    (corner,) = call(collect, [(tile, tile)], order, *parts[:-1], extra, smem=1)
    corners = [corner if r == 1 else lax.ppermute(corner, "row", [(1, r)]) for r in range(rows_axis)]
    free = [flip(near_part, 1) for near_part in near_parts[:-1]]
    parts[-1], corners[2], tied = lax.optimization_barrier((parts[-1], corners[2], near_parts[-1]))
    own_parts = near_parts + free + [flip(tied, 1)]
    (out,) = call(
        functools.partial(finish, rows_axis),
        [(height, tile)],
        order,
        own_order,
        me,
        target,
        block,
        inverses,
        pivots,
        couplings,
        pattern,
        *parts,
        *own_parts,
        *corners,
        smem=3,
        scratch=[
            pltpu.VMEM((height, lead + half), f32),
            pltpu.VMEM((tile, lead), f32),
            pltpu.VMEM((tile, tile), f32),
        ],
    )
    return out


def solution(mesh):
    return jax.shard_map(
        shards,
        mesh=mesh,
        in_specs=(P("row", "col"), P(), P(), P(), P(), P()),
        out_specs=P("row", "col"),
        check_vma=False,
    )
```
